32 devices in a mesh: half: 2 (over core), row: 2 (over x), col: 8 (over z, y).
Axes of the slice: x: 2, y: 2, z: 4, core: 2. Of those that a mesh axis runs over, the one named last changes fastest.
Arguments:
- parent_front: float32 [16384, 16384], P(('half', 'row'), 'col'), may hold values from -6 to 6
- child_blocks: float32 [2, 8192, 8192], P('half', 'row', 'col'), may hold values from -6 to 6
- row_maps: int32 [2, 8192], replicated, may hold values from 0 to 16383, as said below
- inverse_blocks: float32 [4, 128, 128], replicated, may hold values from -0.12 to 0.12
Outputs:
- updated_front: float32 [16384, 16384], P(('half', 'row'), 'col')
- panel_factor: bfloat16 [16384, 512], P(('half', 'row'))
The draws below stay inside these ranges and needn't reach their ends.
Inputs may be any that keep to these rules, and one draw needn't show every extreme that they name: `row_maps`: each row lists 8192 distinct parent rows. In every aligned block of 1024 entries of a row, at most 256 entries fall in one aligned block of 2048 parent rows, and that bound is reached in every such block; in every aligned block of 4096 entries, at most 1536 fall in one aligned block of 4096 parent rows, and that bound is reached in every such block.
All inputs are finite; a program needn't handle non-finite values.
Results may differ from the reference program's by a relative error of at most 0.001.
Values sent between devices are 32-bit elements; how exact they have to be, the bound alone decides.
No kernel may reach another device: no remote copies, remote signals or barrier semaphores. Data moves between devices by JAX's collectives and lax.ppermute only.
A program may use at most 320 MiB of HBM per device.

```python
import jax
import jax.numpy as jnp
from jax import lax

CHILD = 8192
PB = 128
NPB = 4
PARENT = 16384
GROUPS = 4
ROW_SHARD = 4096
COL_SHARD = 1024
COL_LOC = 2048


def child_map(key):
    blocks = CHILD // COL_SHARD
    colgroups = PARENT // COL_LOC
    span = colgroups // GROUPS
    base = COL_SHARD // colgroups
    shards = CHILD // ROW_SHARD
    within = ROW_SHARD // COL_SHARD
    key_hot, key_cold, key_order, key_place = jax.random.split(key, 4)
    hottest = jnp.repeat(jax.random.randint(key_hot, (shards,), 0, colgroups), within)
    offset = jax.random.randint(key_cold, (blocks,), 0, colgroups - span)
    coldest = (hottest // span * span + span + offset) % colgroups
    labels_all = jnp.arange(colgroups, dtype=jnp.int32)
    counts = base + base * (hottest[:, None] == labels_all).astype(jnp.int32) - base * (coldest[:, None] == labels_all).astype(jnp.int32)
    bounds = jnp.cumsum(counts, axis=1)
    position = jnp.arange(COL_SHARD, dtype=jnp.int32)
    sorted_labels = jnp.sum((position[None, :, None] >= bounds[:, None, :]).astype(jnp.int32), axis=2)
    orders = jax.vmap(lambda subkey: jax.random.permutation(subkey, COL_SHARD))(jax.random.split(key_order, blocks))
    labels = jnp.take_along_axis(sorted_labels, orders, axis=1).reshape(CHILD)
    onehot = (labels[:, None] == labels_all).astype(jnp.int32)
    rank = jnp.sum((jnp.cumsum(onehot, axis=0) - onehot) * onehot, axis=1)
    places = jax.vmap(lambda subkey: jax.random.permutation(subkey, COL_LOC))(jax.random.split(key_place, colgroups))
    places = places.astype(jnp.int32)
    target = jnp.where(labels_all == 0, 0, jnp.where(labels_all == colgroups - 1, COL_LOC - 1, places[:, 0]))
    found = jnp.argmax((places == target[:, None]).astype(jnp.int32), axis=1).astype(jnp.int32)
    column = jnp.arange(COL_LOC, dtype=jnp.int32)[None, :]
    places = jnp.where(column == 0, target[:, None], jnp.where(column == found[:, None], places[:, 0:1], places))
    return (labels * COL_LOC + places[labels, rank]).astype(jnp.int32)


def draw_row_maps(key, part):
    first, second = jax.random.split(key)
    return jnp.stack([child_map(first), child_map(second)])


def shard_levels(key, extent, cuts, low, top_value):
    loudness, own = 1.0, jax.random.fold_in(key, 6)
    for dim, blocks in cuts:
        steps = jnp.exp(jax.random.uniform(jax.random.fold_in(own, dim), (blocks,), jnp.float32, low / len(cuts), top_value / len(cuts)))
        loudness = loudness * jnp.repeat(steps, extent[dim] // blocks).reshape([-1 if axis == dim else 1 for axis in range(len(extent))])
    return loudness


def gaussian(stream_key, extent, width, most, cuts=(), kind=jnp.bfloat16):
    entries = width * jax.random.normal(stream_key, extent, jnp.float32)
    if cuts:
        entries = entries * shard_levels(stream_key, extent, cuts, -0.22, 0.18)
    return jnp.clip(entries, -most, most).astype(kind)


def setup_inputs(seed: int = 0) -> dict:
    arg_keys = jax.random.split(jax.random.key(seed), 5)
    return {
        "parent_front": gaussian(arg_keys[0], (PARENT, PARENT), 1.0, 6.0, ((0, 4), (1, 8)), jnp.float32),
        "child_blocks": gaussian(arg_keys[1], (2, CHILD, CHILD), 1.0, 6.0, ((0, 2), (1, 2), (2, 8)), jnp.float32),
        "row_maps": draw_row_maps(jax.random.fold_in(arg_keys[4], 71), 0),
        "inverse_blocks": gaussian(arg_keys[3], (NPB, PB, PB), 0.02, 0.12, (), jnp.float32),
    }


def highest_dot(left, right):
    return jnp.dot(left, right, precision=lax.Precision.HIGHEST, preferred_element_type=jnp.float32)


def reference(parent_front, child_blocks, row_maps, inverse_blocks):
    assembled = parent_front
    for child in range(2):
        spread = jnp.zeros((CHILD, PARENT), jnp.float32).at[:, row_maps[child]].set(child_blocks[child])
        assembled = assembled.at[row_maps[child]].add(spread)
    factors = []
    for block in range(NPB):
        current = assembled[:, block * PB:(block + 1) * PB]
        if block > 0:
            earlier = jnp.concatenate(factors, axis=1)
            current = current - highest_dot(earlier, earlier[block * PB:(block + 1) * PB].T)
        factors.append(highest_dot(current, jnp.tril(inverse_blocks[block]).T))
    factor = jnp.concatenate(factors, axis=1)
    updated_front = assembled - highest_dot(factor, factor.T)
    return updated_front, factor.astype(jnp.bfloat16)
```

```python
import functools

import jax
import jax.numpy as jnp
from jax import lax
from jax.experimental import pallas as pl
from jax.experimental.pallas import tpu as pltpu
from jax.sharding import PartitionSpec as P

LANES = 128
CHUNKS = 2
TILE = 256
SLAB = 64


def from_root(block, axis, holder):
    block = jnp.where(lax.axis_index(axis) == holder, block, jnp.zeros_like(block))
    return lax.psum(block, axis)


def highest_outer(left, right):
    return lax.dot_general(
        left,
        right,
        (((1,), (1,)), ((), ())),
        precision=lax.Precision.HIGHEST,
        preferred_element_type=jnp.float32,
    )


def ranks(targets, count):
    onehot = (targets[..., None] == jnp.arange(count, dtype=jnp.int32)).astype(jnp.int32)
    before = jnp.cumsum(onehot, axis=-2) - onehot
    return jnp.sum(before * onehot, axis=-1)


def row_tables(row_maps, row_loc, groups, cap_rows, my_group):
    parent_rows = row_maps.reshape(groups, -1)
    targets = parent_rows // row_loc
    slots = ranks(targets, groups)
    sources = jnp.arange(groups, dtype=jnp.int32)[:, None]
    where_at = jnp.where(targets == my_group, sources * cap_rows + slots, groups * cap_rows)
    table = (
        jnp.full((groups * cap_rows,), row_loc, jnp.int32)
        .at[where_at.reshape(-1)]
        .set((parent_rows % row_loc).reshape(-1), mode="drop")
    )
    send_at = targets[my_group] * cap_rows + slots[my_group]
    return (send_at, table)


def col_tables(row_maps, col_loc, n_col, cap_cols, my_col):
    parent_cols = row_maps.reshape(2, n_col, -1)
    targets = parent_cols // col_loc
    slots = ranks(targets, n_col)
    sources = jnp.arange(n_col, dtype=jnp.int32)[None, :, None]
    where_at = jnp.where(targets == my_col, sources * cap_cols + slots, n_col * cap_cols)
    child_index = jnp.broadcast_to(jnp.arange(2, dtype=jnp.int32)[:, None, None], where_at.shape)
    table = (
        jnp.full((2, n_col * cap_cols), col_loc, jnp.int32)
        .at[child_index, where_at]
        .set(parent_cols % col_loc, mode="drop")
    )
    send_at = targets[:, my_col] * cap_cols + slots[:, my_col]
    return (send_at, table)


def row_pack(values, send_at, total):
    return jnp.zeros((total, values.shape[1]), values.dtype).at[send_at].set(values)


def col_pack(values, send_at, total):
    return jnp.zeros((values.shape[0], total), values.dtype).at[:, send_at].set(values)


def round_up(value, step):
    return -(-value // step) * step


def split(values):
    high = lax.reduce_precision(values, 8, 7)
    return high.astype(jnp.bfloat16), (values - high).astype(jnp.bfloat16)


def place_kernel(parts, starts, rounds, row_tab, col_tab, base, *refs):
    landed, out, spread, rows_high, rows_low = refs[:parts], *refs[parts:]
    tile = pl.program_id(0)
    height, width = base.shape
    n_src, n_col, window, lanes = landed[0].shape
    packed = n_col * lanes

    @pl.when(tile == 0)
    def _():
        column = lax.broadcasted_iota(jnp.int32, (lanes, width), 1)

        def fill(at, carry):
            rows = pl.ds(pl.multiple_of(at * lanes, lanes), lanes)
            spread[rows, :] = (col_tab[rows, :] == column).astype(jnp.bfloat16)
            return carry

        lax.fori_loop(0, 2 * n_col, fill, 0)

    total = base[...]
    slab = min(SLAB, window)
    for child in range(2):
        rows_high[...] = jnp.zeros_like(rows_high)
        rows_low[...] = jnp.zeros_like(rows_low)

        def step(turn, carry):
            values, hits = [], []
            for shard in range(n_src // 2):
                source = child * (n_src // 2) + shard
                for part in range(parts):
                    first = starts[(tile * n_src + source) * parts + part] + turn * slab
                    at = pl.multiple_of(jnp.minimum(first, window - slab), 8)
                    rows = pl.ds(at, slab)
                    values.append(jnp.concatenate([landed[part][source, j, rows, :] for j in range(n_col)], axis=1))
                    index = at + lax.broadcasted_iota(jnp.int32, (slab, height), 0)
                    target = tile * height + lax.broadcasted_iota(jnp.int32, (slab, height), 1)
                    hits.append(((row_tab[source * parts + part, rows, :] == target) & (index >= first)).astype(jnp.bfloat16))
            value = jnp.concatenate(values, axis=0)
            hit = jnp.concatenate(hits, axis=0)
            high = value.astype(jnp.bfloat16)
            low = (value - high.astype(jnp.float32)).astype(jnp.bfloat16)
            dims = (((0,), (0,)), ((), ()))
            rows_high[...] += lax.dot_general(hit, high, dims, preferred_element_type=jnp.float32)
            rows_low[...] += lax.dot_general(hit, low, dims, preferred_element_type=jnp.float32)
            return carry

        lax.fori_loop(0, rounds[tile * 2 + child], step, 0)
        wide = spread[child * packed : (child + 1) * packed, :]
        total += jnp.dot(rows_high[...].astype(jnp.bfloat16), wide, preferred_element_type=jnp.float32)
        total += jnp.dot(rows_low[...].astype(jnp.bfloat16), wide, preferred_element_type=jnp.float32)
    out[...] = total


def place(base, landed, row_tab, col_tab):
    height, width = base.shape
    parts = len(landed)
    n_src, n_col, window, lanes = landed[0].shape
    packed = n_col * lanes
    tile = min(TILE, height)
    tiles = height // tile
    slab = min(SLAB, window)
    edges = jnp.arange(tiles + 1, dtype=jnp.int32) * tile
    inside = row_tab >= 0
    below = jnp.sum((row_tab[..., None, :] < edges[:, None]).astype(jnp.int32), axis=-1)
    past = jnp.sum((jnp.where(inside, row_tab, height)[..., None, :] < edges[:, None]).astype(jnp.int32), axis=-1)
    ahead = jnp.argmax(inside.astype(jnp.int32), axis=-1)[..., None]
    first = (ahead + past[..., :-1]) // 8 * 8
    last = ahead + past[..., 1:]
    count = jnp.where(past[..., 1:] > past[..., :-1], (last - first + slab - 1) // slab, 0)
    rounds = jnp.max(count.reshape(2, -1, tiles), axis=1).T.reshape(-1)
    starts = jnp.moveaxis(first, -1, 0).reshape(-1)
    whole = lambda shape: pl.BlockSpec(shape, lambda *_: (0,) * len(shape), pipeline_mode=pl.Buffered(1))
    spec = pltpu.PrefetchScalarGridSpec(
        num_scalar_prefetch=2,
        grid=(tiles,),
        in_specs=[
            whole((n_src * parts, window, 1)),
            whole((2 * packed, 1)),
            pl.BlockSpec((tile, width), lambda i, *_: (i, 0)),
        ]
        + [whole((n_src, n_col, window, lanes))] * parts,
        out_specs=pl.BlockSpec((tile, width), lambda i, *_: (i, 0)),
        scratch_shapes=[
            pltpu.VMEM((2 * packed, width), jnp.bfloat16),
            pltpu.VMEM((tile, packed), jnp.float32),
            pltpu.VMEM((tile, packed), jnp.float32),
        ],
    )
    return pl.pallas_call(
        functools.partial(place_kernel, parts),
        grid_spec=spec,
        out_shape=jax.ShapeDtypeStruct(base.shape, base.dtype),
        compiler_params=pltpu.CompilerParams(vmem_limit_bytes=60 * 2**20),
        cost_estimate=pl.CostEstimate(
            flops=8 * height * packed * width, bytes_accessed=8 * height * width + 4 * parts * n_src * packed * window, transcendentals=0
        ),
        name="place",
    )(starts, rounds, row_tab.reshape(n_src * parts, window, 1), col_tab.reshape(-1, 1), base, *landed)


def column_plan(row_maps, col_loc, n_col, share):
    parent_cols = row_maps.reshape(2, n_col, -1)
    owner = parent_cols // col_loc
    size = owner.shape[-1]
    earlier = jnp.arange(size)[:, None] > jnp.arange(size)[None, :]
    same = (owner[..., :, None] == owner[..., None, :]) & earlier
    rank = jnp.sum(same.astype(jnp.int32), axis=-1)
    over = rank >= share
    over_rank = jnp.sum((over[..., None, :] & earlier).astype(jnp.int32), axis=-1)
    most = jnp.max(jnp.sum(over.astype(jnp.int32), axis=-1))
    send = jnp.where(over, -1, owner * share + rank)
    send_over = jnp.where(over, over_rank, -1)
    return parent_cols, owner, rank, send, send_over, most


def seen_from(here, parent_cols, slot, col_loc, count):
    hit = (slot[..., None] == jnp.arange(count, dtype=jnp.int32)) & here[..., None]
    return jnp.sum(jnp.where(hit, parent_cols[..., None] % col_loc + 1, 0), axis=2) - 1


def even(parent_front, child_blocks, row_maps, plan):
    row_loc, col_loc = parent_front.shape
    child_rows, child_cols = child_blocks.shape[1:]
    n_row, n_col = lax.axis_size("row"), lax.axis_size("col")
    n_half = lax.axis_size("half")
    groups = n_half * n_row
    my_child = lax.axis_index("half")
    my_group = my_child * n_row + lax.axis_index("row")
    my_col = lax.axis_index("col")
    cap_rows = n_col // n_row * (child_cols // groups + child_cols // n_col)
    share = child_cols // n_col
    parent_cols, owner, rank, send, send_over, _ = plan
    here = owner == my_col
    col_tab = seen_from(here, parent_cols, jnp.where(send >= 0, rank, -1), col_loc, share)
    over_tab = seen_from(here, parent_cols, send_over, col_loc, share)
    my_send = lax.dynamic_index_in_dim(send[my_child], my_col, 0, keepdims=False)
    my_over = lax.dynamic_index_in_dim(send_over[my_child], my_col, 0, keepdims=False)
    pick = (my_send[:, None] == jnp.arange(n_col * share, dtype=jnp.int32)).astype(jnp.bfloat16)
    pick_over = (my_over[:, None] == jnp.arange(share, dtype=jnp.int32)).astype(jnp.bfloat16)

    blocks = row_maps.reshape(groups, child_rows)
    order = jnp.sort(blocks * child_rows + jnp.arange(child_rows, dtype=jnp.int32), axis=1)
    sorted_row = order // child_rows
    sorted_from = order % child_rows
    edges = jnp.arange(groups, dtype=jnp.int32) * row_loc
    begin = jnp.sum((blocks[:, None, :] < edges[:, None]).astype(jnp.int32), axis=-1)

    def window(chunks, chunk):
        size = min(round_up(-(-cap_rows // chunks), 8) + 8, child_rows // chunks)
        first = jnp.maximum(begin - chunk + chunks - 1, 0) // chunks
        first = jnp.minimum(first // 8 * 8, child_rows // chunks - size)
        return size, first

    def table(chunks, chunk):
        size, first = window(chunks, chunk)
        rows = sorted_row[:, chunk::chunks]
        mine = lax.dynamic_index_in_dim(first, my_group, 1, keepdims=False)
        rows = jnp.stack([lax.dynamic_slice_in_dim(rows[s], mine[s], size, 0) for s in range(groups)])
        local = rows - my_group * row_loc
        return jnp.where((local >= 0) & (local < row_loc), local, -1)

    def row_exchange(values, chunks, chunk, axis):
        size, first = window(chunks, chunk)
        mine = lax.dynamic_index_in_dim(first, my_group, 0, keepdims=False)
        out = jnp.stack([lax.dynamic_slice_in_dim(values, mine[t], size, axis) for t in range(groups)])
        return lax.all_to_all(out, ("half", "row"), split_axis=0, concat_axis=0, tiled=True)

    from_row = lax.dynamic_index_in_dim(sorted_from, my_group, 0, keepdims=False)
    mine = child_blocks[0]
    taken = [mine[from_row[chunk::CHUNKS]] for chunk in range(CHUNKS)]
    pairs = [split(values) for values in taken]

    def packed(pair, choice, form):
        high, low = pair
        return jnp.einsum(form, high, choice, preferred_element_type=jnp.float32) + jnp.einsum(
            form, low, choice, preferred_element_type=jnp.float32
        )

    wide_pick = pick.reshape(child_cols, n_col, share)
    arrived = []
    for chunk in range(CHUNKS):
        moved = packed(pairs[chunk], wide_pick, "rk,kdu->dru")
        arrived.append(lax.all_to_all(moved, "col", split_axis=0, concat_axis=0, tiled=True))
    over = jnp.stack([packed(pair, pick_over, "rk,ku->ru") for pair in pairs], axis=1).reshape(child_rows, share)
    over = row_exchange(over, 1, 0, 0)
    over = lax.all_gather(over, "col", axis=1)
    landed = [row_exchange(arrived[chunk], CHUNKS, chunk, 1) for chunk in range(CHUNKS)]
    tables = jnp.stack([table(CHUNKS, chunk) for chunk in range(CHUNKS)], axis=1)
    first = place(parent_front, [over], table(1, 0)[:, None], over_tab)
    return place(first, landed, tables, col_tab)


def general(parent_front, child_blocks, row_maps):
    row_loc, col_loc = parent_front.shape
    child_rows, child_cols = (child_blocks.shape[1], child_blocks.shape[2])
    n_row = lax.axis_size("row")
    n_col = lax.axis_size("col")
    groups = lax.axis_size("half") * n_row
    my_child = lax.axis_index("half")
    my_group = my_child * n_row + lax.axis_index("row")
    my_col = lax.axis_index("col")
    cap_cols = 2 * child_cols // n_col
    cap_rows = n_col // n_row * (child_cols // groups + child_cols // n_col)
    slab_rows = n_row * cap_rows
    row_send, row_table = row_tables(row_maps, row_loc, groups, cap_rows, my_group)
    col_send, col_table = col_tables(row_maps, col_loc, n_col, cap_cols, my_col)
    mine = child_blocks[0]
    moved = col_pack(mine, col_send[my_child], n_col * cap_cols)
    arrived = lax.all_to_all(moved, "col", split_axis=1, concat_axis=1, tiled=True)
    outgoing = row_pack(arrived, row_send, groups * cap_rows)
    landed = lax.all_to_all(
        outgoing, ("half", "row"), split_axis=0, concat_axis=0, tiled=True
    ).reshape(2, slab_rows, n_col * cap_cols)
    row_dest = row_table.reshape(2, slab_rows)
    assembled = parent_front
    for child in range(2):
        spread = (
            jnp.zeros((slab_rows, col_loc), jnp.float32)
            .at[:, col_table[child]]
            .add(landed[child], mode="drop")
        )
        assembled = assembled.at[row_dest[child]].add(spread, mode="drop")
    return assembled


def local(parent_front, child_blocks, row_maps, inverse_blocks):
    row_loc, col_loc = parent_front.shape
    n_col = lax.axis_size("col")
    n_row = lax.axis_size("row")
    groups = lax.axis_size("half") * n_row
    my_col = lax.axis_index("col")
    share = child_blocks.shape[2] // n_col
    if share % LANES:
        assembled = general(parent_front, child_blocks, row_maps)
    else:
        plan = column_plan(row_maps, col_loc, n_col, share)
        assembled = lax.cond(
            plan[-1] <= share,
            lambda parent, child: even(parent, child, row_maps, plan),
            lambda parent, child: general(parent, child, row_maps),
            parent_front,
            child_blocks,
        )
    width = inverse_blocks.shape[1]
    count = inverse_blocks.shape[0]
    span = n_col // groups
    root = my_col // span
    start = my_col % span * col_loc
    inverses = jnp.tril(inverse_blocks)
    at_root = (lax.axis_index("half") == 0) & (lax.axis_index("row") == 0)
    corner = assembled[: count * width, : count * width]
    corner = lax.psum(jnp.where(at_root, corner, jnp.zeros_like(corner)), ("half", "row"))

    def panel(columns, tops):
        factors = []
        for block in range(count):
            current = columns[:, block * width : (block + 1) * width]
            if block > 0:
                earlier = jnp.concatenate(factors, axis=1)
                above = (earlier if tops is None else tops)[block * width : (block + 1) * width, : block * width]
                current = current - highest_outer(earlier, above)
            factors.append(highest_outer(current, inverses[block]))
        return jnp.concatenate(factors, axis=1)

    tops = panel(corner, None)
    local_factor = panel(assembled[:, : count * width], tops)
    factor_rows = from_root(local_factor, "col", 0)
    piece = lax.dynamic_slice_in_dim(factor_rows, start, col_loc, 0)
    factor_cols = from_root(piece, ("half", "row"), root)
    updated_front = assembled - highest_outer(factor_rows, factor_cols)
    return (updated_front, factor_rows.astype(jnp.bfloat16))


def solution(mesh):
    in_specs = (P(("half", "row"), "col"), P("half", "row", "col"), P(), P())
    out_specs = (P(("half", "row"), "col"), P(("half", "row"), None))
    return jax.shard_map(local, mesh=mesh, in_specs=in_specs, out_specs=out_specs, check_vma=False)
```

```python
import functools

import jax
import jax.numpy as jnp
from jax import lax
from jax.experimental import pallas as pl
from jax.experimental.pallas import tpu as pltpu
from jax.sharding import PartitionSpec as P

LANES = 128
CHUNKS = 4
TILE = 256
SLAB = 32
WIDE = 512


def from_root(block, axis, holder):
    block = jnp.where(lax.axis_index(axis) == holder, block, jnp.zeros_like(block))
    return lax.psum(block, axis)


def highest_outer(left, right):
    return lax.dot_general(
        left,
        right,
        (((1,), (1,)), ((), ())),
        precision=lax.Precision.HIGHEST,
        preferred_element_type=jnp.float32,
    )


def ranks(targets, count):
    onehot = (targets[..., None] == jnp.arange(count, dtype=jnp.int32)).astype(jnp.int32)
    before = jnp.cumsum(onehot, axis=-2) - onehot
    return jnp.sum(before * onehot, axis=-1)


def row_tables(row_maps, row_loc, groups, cap_rows, my_group):
    parent_rows = row_maps.reshape(groups, -1)
    targets = parent_rows // row_loc
    slots = ranks(targets, groups)
    sources = jnp.arange(groups, dtype=jnp.int32)[:, None]
    where_at = jnp.where(targets == my_group, sources * cap_rows + slots, groups * cap_rows)
    table = (
        jnp.full((groups * cap_rows,), row_loc, jnp.int32)
        .at[where_at.reshape(-1)]
        .set((parent_rows % row_loc).reshape(-1), mode="drop")
    )
    send_at = targets[my_group] * cap_rows + slots[my_group]
    return (send_at, table)


def col_tables(row_maps, col_loc, n_col, cap_cols, my_col):
    parent_cols = row_maps.reshape(2, n_col, -1)
    targets = parent_cols // col_loc
    slots = ranks(targets, n_col)
    sources = jnp.arange(n_col, dtype=jnp.int32)[None, :, None]
    where_at = jnp.where(targets == my_col, sources * cap_cols + slots, n_col * cap_cols)
    child_index = jnp.broadcast_to(jnp.arange(2, dtype=jnp.int32)[:, None, None], where_at.shape)
    table = (
        jnp.full((2, n_col * cap_cols), col_loc, jnp.int32)
        .at[child_index, where_at]
        .set(parent_cols % col_loc, mode="drop")
    )
    send_at = targets[:, my_col] * cap_cols + slots[:, my_col]
    return (send_at, table)


def row_pack(values, send_at, total):
    return jnp.zeros((total, values.shape[1]), values.dtype).at[send_at].set(values)


def col_pack(values, send_at, total):
    return jnp.zeros((values.shape[0], total), values.dtype).at[:, send_at].set(values)


def round_up(value, step):
    return -(-value // step) * step


def split(values):
    high = lax.reduce_precision(values, 8, 7)
    return high.astype(jnp.bfloat16), (values - high).astype(jnp.bfloat16)


def window_kernel(count, starts, values, *refs):
    outs, sems = refs[:-1], refs[-1]
    size = outs[0].shape[1]
    copies = []
    for way, out in enumerate(outs):
        for at in range(count):
            first = pl.multiple_of(starts[way * count + at], 8)
            copies.append(pltpu.make_async_copy(values.at[at, pl.ds(first, size), :], out.at[at], sems.at[way * count + at]))
    for copy in copies:
        copy.start()
    for copy in copies:
        copy.wait()


def windows(values, starts, size):
    count, _, lanes = values.shape
    ways = starts.shape[0]
    anywhere = pl.BlockSpec(memory_space=pl.ANY)
    return pl.pallas_call(
        functools.partial(window_kernel, count),
        in_specs=[pl.BlockSpec(memory_space=pltpu.SMEM), anywhere],
        out_specs=[anywhere] * ways,
        out_shape=[jax.ShapeDtypeStruct((count, size, lanes), values.dtype)] * ways,
        scratch_shapes=[pltpu.SemaphoreType.DMA((ways * count,))],
        cost_estimate=pl.CostEstimate(flops=0, bytes_accessed=8 * ways * count * size * lanes, transcendentals=0),
        name="windows",
    )(starts.reshape(-1), values)


def place_kernel(form, starts, rounds, flags, row_tab, col_tab, base, *refs):
    parts, n_src, n_col, gates, n_landed, update = form
    landed = refs[:n_landed]
    extra = refs[n_landed : n_landed + 2 * update]
    out, spread, rows_high, rows_low = refs[n_landed + 2 * update :]
    tile = pl.program_id(0)
    height, width = base.shape
    window, lanes = landed[0].shape[-2:]
    packed = n_col * lanes
    slab = min(SLAB, window)
    wide = min(WIDE, width)

    def read(source, part, j, rows):
        if len(landed[0].shape) == 5:
            return landed[0][j, source, part, rows, :]
        if n_landed == n_src:
            return landed[source][part, rows, :]
        return landed[part * n_src + source][j, rows, :]

    @pl.when(tile == 0)
    def _():
        column = lax.broadcasted_iota(jnp.int32, (lanes, width), 1)

        def fill(at, carry):
            rows = pl.ds(pl.multiple_of(at * lanes, lanes), lanes)
            spread[rows, :] = (col_tab[rows, :] == column).astype(jnp.bfloat16)
            return carry

        lax.fori_loop(0, 2 * n_col, fill, 0)

    for child in range(2):
        mine = slice(child * packed, (child + 1) * packed)
        rows_high[:, mine] = jnp.zeros((height, packed), jnp.float32)
        rows_low[:, mine] = jnp.zeros((height, packed), jnp.float32)

        def step(turn, carry):
            values, hits = [], []
            for source in range(child * n_src // 2, (child + 1) * n_src // 2):
                for part in range(parts):
                    first = starts[(tile * n_src + source) * parts + part] + turn * slab
                    at = pl.multiple_of(jnp.minimum(first, window - slab), 8)
                    rows = pl.ds(at, slab)
                    values.append(jnp.concatenate([read(source, part, j, rows) for j in range(n_col)], axis=1))
                    index = at + lax.broadcasted_iota(jnp.int32, (slab, height), 0)
                    target = tile * height + lax.broadcasted_iota(jnp.int32, (slab, height), 1)
                    hits.append(((row_tab[source * parts + part, rows, :] == target) & (index >= first)).astype(jnp.float32))
            value = jnp.concatenate(values, axis=0)
            hit = jnp.concatenate(hits, axis=0).astype(jnp.bfloat16)
            high = value.astype(jnp.bfloat16)
            low = (value - high.astype(jnp.float32)).astype(jnp.bfloat16)
            dims = (((0,), (0,)), ((), ()))
            rows_high[:, mine] += lax.dot_general(hit, high, dims, preferred_element_type=jnp.float32)
            rows_low[:, mine] += lax.dot_general(hit, low, dims, preferred_element_type=jnp.float32)
            return carry

        lax.fori_loop(0, rounds[tile * 2 + child], step, 0)

    def matmuls(at, carry):
        cols = pl.ds(pl.multiple_of(at * wide, wide), wide)
        if not gates:
            right = spread[:, cols]
            total = base[:, cols]
            total += jnp.dot(rows_high[...].astype(jnp.bfloat16), right, preferred_element_type=jnp.float32)
            total += jnp.dot(rows_low[...].astype(jnp.bfloat16), right, preferred_element_type=jnp.float32)
            if update:
                left, above = extra
                total += lax.dot_general(
                    left[...], above[cols, :], (((1,), (1,)), ((), ())), preferred_element_type=jnp.float32
                )
            out[:, cols] = total
            return carry
        out[:, cols] = base[:, cols]
        depth = 2 * packed // gates
        for gate in range(gates):

            @pl.when(flags[gate] > 0)
            def _():
                part = slice(gate * depth, (gate + 1) * depth)
                right = spread[part, cols]
                total = jnp.dot(rows_high[:, part].astype(jnp.bfloat16), right, preferred_element_type=jnp.float32)
                total += jnp.dot(rows_low[:, part].astype(jnp.bfloat16), right, preferred_element_type=jnp.float32)
                out[:, cols] += total

        return carry

    lax.fori_loop(0, width // wide, matmuls, 0)


def place(base, landed, row_tab, col_tab, gates=0, factor=None):
    height, width = base.shape
    n_src, parts, window = row_tab.shape
    n_col, lanes = col_tab.shape[1:]
    packed = n_col * lanes
    tile = min(TILE, height)
    tiles = height // tile
    slab = min(SLAB, window)
    edges = jnp.arange(tiles + 1, dtype=jnp.int32) * tile
    inside = row_tab >= 0
    past = jnp.sum((jnp.where(inside, row_tab, height)[..., None, :] < edges[:, None]).astype(jnp.int32), axis=-1)
    ahead = jnp.argmax(inside.astype(jnp.int32), axis=-1)[..., None]
    first = (ahead + past[..., :-1]) // 8 * 8
    last = ahead + past[..., 1:]
    count = jnp.where(past[..., 1:] > past[..., :-1], (last - first + slab - 1) // slab, 0)
    rounds = jnp.max(count.reshape(2, -1, tiles), axis=1)
    flags = jnp.zeros((1,), jnp.int32)
    if gates:
        flags = jnp.any((col_tab >= 0).reshape(gates, -1), axis=1).astype(jnp.int32)
        rounds = rounds * jnp.max(flags.reshape(2, -1), axis=1)[:, None]
    starts = jnp.moveaxis(first, -1, 0).reshape(-1)
    extra = [] if factor is None else list(factor)
    whole = lambda shape: pl.BlockSpec(shape, lambda *_: (0,) * len(shape), pipeline_mode=pl.Buffered(1))
    block = lambda shape: pl.BlockSpec(shape, lambda i, *_: (i, 0))
    spec = pltpu.PrefetchScalarGridSpec(
        num_scalar_prefetch=3,
        grid=(tiles,),
        in_specs=[whole((n_src * parts, window, 1)), whole((2 * packed, 1)), block((tile, width))]
        + [whole(array.shape) for array in landed]
        + ([block((tile, extra[0].shape[1])), whole(extra[1].shape)] if extra else []),
        out_specs=block((tile, width)),
        scratch_shapes=[
            pltpu.VMEM((2 * packed, width), jnp.bfloat16),
            pltpu.VMEM((tile, 2 * packed), jnp.float32),
            pltpu.VMEM((tile, 2 * packed), jnp.float32),
        ],
    )
    return pl.pallas_call(
        functools.partial(place_kernel, (parts, n_src, n_col, gates, len(landed), 1 if extra else 0)),
        grid_spec=spec,
        out_shape=jax.ShapeDtypeStruct(base.shape, base.dtype),
        compiler_params=pltpu.CompilerParams(vmem_limit_bytes=62 * 2**20),
        cost_estimate=pl.CostEstimate(
            flops=8 * height * packed * width, bytes_accessed=8 * height * width + 4 * parts * n_src * packed * window, transcendentals=0
        ),
        name="place",
    )(starts, rounds.T.reshape(-1), flags, row_tab.reshape(n_src * parts, window, 1), col_tab.reshape(-1, 1), base, *landed, *extra)


def earlier_count(marks):
    size = marks.shape[-2]
    before = (jnp.arange(size)[:, None] > jnp.arange(size)[None, :]).astype(jnp.bfloat16)
    counts = jnp.einsum("ab,csbn->csan", before, marks.astype(jnp.bfloat16), preferred_element_type=jnp.float32)
    return counts.astype(jnp.int32)


def column_plan(row_maps, col_loc, n_col, share, panel):
    parent_cols = row_maps.reshape(2, n_col, -1)
    owner = parent_cols // col_loc
    onehot = owner[..., None] == jnp.arange(n_col, dtype=jnp.int32)
    rank = jnp.sum(jnp.where(onehot, earlier_count(onehot), 0), axis=-1)
    over = rank >= share
    early = parent_cols < panel
    marks = jnp.stack([over, early], axis=-1)
    order = earlier_count(marks)
    most = jnp.max(jnp.sum(marks.astype(jnp.int32), axis=2))
    send = jnp.where(over, -1, rank)
    send_over = jnp.where(over, order[..., 0], -1)
    send_early = jnp.where(early, order[..., 1], -1)
    return parent_cols, owner, send, send_over, send_early, most


def seen_from(here, parent_cols, slot, col_loc, count):
    hit = (slot[..., None] == jnp.arange(count, dtype=jnp.int32)) & here[..., None]
    return jnp.sum(jnp.where(hit, parent_cols[..., None] % col_loc + 1, 0), axis=2) - 1


def panel_of(columns, inverses, tops):
    count, width = inverses.shape[:2]
    factors = []
    for block in range(count):
        current = columns[:, block * width : (block + 1) * width]
        if block > 0:
            earlier = jnp.concatenate(factors, axis=1)
            above = (earlier if tops is None else tops)[block * width : (block + 1) * width, : block * width]
            current = current - highest_outer(earlier, above)
        factors.append(highest_outer(current, inverses[block]))
    return jnp.concatenate(factors, axis=1)


def even(parent_front, child_blocks, row_maps, inverse_blocks, plan):
    row_loc, col_loc = parent_front.shape
    child_rows, child_cols = child_blocks.shape[1:]
    n_row, n_col = lax.axis_size("row"), lax.axis_size("col")
    groups = lax.axis_size("half") * n_row
    my_child = lax.axis_index("half")
    my_group = my_child * n_row + lax.axis_index("row")
    my_col = lax.axis_index("col")
    cap_rows = n_col // n_row * (child_cols // groups + child_cols // n_col)
    share = child_cols // n_col
    panel = inverse_blocks.shape[0] * inverse_blocks.shape[1]
    parent_cols, owner, send, send_over, send_early, _ = plan
    pick_at = lambda array, at: lax.dynamic_index_in_dim(array, at, 0, keepdims=False)
    here = owner == my_col
    ordered = lambda tab: jnp.stack([pick_at(tab, my_child), pick_at(tab, 1 - my_child)])
    col_tab = ordered(seen_from(here, parent_cols, send, col_loc, share))
    over_tab = ordered(seen_from(here, parent_cols, send_over, col_loc, share))
    at_col = lambda array: lax.dynamic_slice_in_dim(array, my_col, 1, 1)
    early_cols = at_col(parent_cols)
    early_tab = ordered(seen_from(early_cols >= 0, early_cols, at_col(send_early), panel, share))
    own = lambda array: pick_at(pick_at(array, my_child), my_col)
    slots = jnp.arange(share, dtype=jnp.int32)
    owners = jnp.arange(n_col, dtype=jnp.int32)
    pick = ((own(owner)[:, None, None] == owners[:, None]) & (own(send)[:, None, None] == slots)).astype(jnp.bfloat16)
    pick_first = jnp.stack([own(send_over)[:, None] == slots, own(send_early)[:, None] == slots], axis=1).astype(jnp.bfloat16)

    blocks = row_maps.reshape(groups, child_rows)
    order = jnp.sort(blocks * child_rows + jnp.arange(child_rows, dtype=jnp.int32), axis=1)
    sorted_row = jnp.swapaxes((order // child_rows).reshape(groups, -1, CHUNKS), 1, 2)
    from_row = pick_at(order, my_group) % child_rows
    edges = jnp.arange(groups, dtype=jnp.int32) * row_loc
    begin = jnp.sum((blocks[:, None, :] < edges[:, None]).astype(jnp.int32), axis=-1)
    length = child_rows // CHUNKS
    size = min(round_up(-(-cap_rows // CHUNKS), 8) + 8, length)
    chunks = jnp.arange(CHUNKS, dtype=jnp.int32)
    first = jnp.maximum(begin[..., None] - chunks + CHUNKS - 1, 0) // CHUNKS
    first = jnp.minimum(first // 8 * 8, length - size)
    ways = jnp.bitwise_xor(my_group, jnp.arange(groups, dtype=jnp.int32))
    starts = pick_at(first, my_group)[ways]
    opening = lax.dynamic_index_in_dim(first, my_group, 1, keepdims=False)

    def table(source):
        rows, opens = pick_at(sorted_row, source), pick_at(opening, source)
        return jnp.stack([lax.dynamic_slice_in_dim(rows[chunk], opens[chunk], size, 0) for chunk in range(CHUNKS)])

    row_tab = jnp.stack([table(ways[way]) for way in range(groups)]) - my_group * row_loc
    row_tab = jnp.where((row_tab >= 0) & (row_tab < row_loc), row_tab, -1)

    def row_exchange(pieces):
        swaps = [[(group, group ^ way) for group in range(groups)] for way in range(groups)]
        return [pieces[0]] + [lax.ppermute(pieces[way], ("half", "row"), swaps[way]) for way in range(1, groups)]

    def packed(pair, choice):
        form = "rk,kdu->dru"
        return jnp.einsum(form, pair[0], choice, preferred_element_type=jnp.float32) + jnp.einsum(
            form, pair[1], choice, preferred_element_type=jnp.float32
        )

    mine = child_blocks[0]
    pairs = [split(mine[from_row[chunk::CHUNKS]]) for chunk in range(CHUNKS)]
    ahead = jnp.concatenate([packed(pair, pick_first) for pair in pairs], axis=0)
    ahead = windows(ahead, jnp.repeat(starts, 2, axis=1), size)
    ahead = row_exchange(ahead)
    ahead = [piece.reshape(CHUNKS, 2, size, share) for piece in ahead]
    over = jnp.stack([piece[:, 0] for piece in ahead])
    early = [piece[:, 1] for piece in ahead]

    front = parent_front[:, :panel]
    front = place(jnp.where(my_col == 0, front, jnp.zeros_like(front)), early, row_tab, early_tab)
    front = lax.psum(front, "col")
    over = lax.all_gather(over, "col", axis=0)

    landed = []
    for chunk in range(CHUNKS):
        moved = lax.all_to_all(packed(pairs[chunk], pick), "col", split_axis=0, concat_axis=0, tiled=True)
        pieces = windows(moved, jnp.repeat(starts[:, chunk : chunk + 1], n_col, axis=1), size)
        landed += row_exchange(pieces)

    corner = front[:panel]
    sent = [lax.ppermute(corner, ("half", "row"), [(0, way)]) for way in range(1, groups)]
    corner = jnp.where(my_group == 0, corner, functools.reduce(jnp.add, sent))
    inverses = jnp.tril(inverse_blocks)
    factor_rows = panel_of(front, inverses, panel_of(corner, inverses, None))
    span = n_col // groups
    piece = lax.dynamic_slice_in_dim(factor_rows, my_col % span * col_loc, col_loc, 0)
    spots = [(col // span * n_col + col, col) for col in range(n_col)]
    sent = [
        lax.ppermute(piece, ("half", "row", "col"), [(at, ((at // n_col) ^ way) * n_col + col) for at, col in spots])
        for way in range(1, groups)
    ]
    factor_cols = jnp.where(my_group == my_col // span, piece, functools.reduce(jnp.add, sent))
    row_high, row_low = split(-factor_rows)
    col_high, col_low = split(factor_cols)
    left = jnp.concatenate([row_high, row_high, row_low], axis=1)
    above = jnp.concatenate([col_high, col_low, col_high], axis=1)

    first_sum = place(parent_front, [over], row_tab, over_tab, gates=4)
    updated = place(first_sum, landed, row_tab, col_tab, factor=(left, above))
    return updated, factor_rows.astype(jnp.bfloat16)


def general(parent_front, child_blocks, row_maps, inverse_blocks):
    row_loc, col_loc = parent_front.shape
    child_rows, child_cols = (child_blocks.shape[1], child_blocks.shape[2])
    n_row = lax.axis_size("row")
    n_col = lax.axis_size("col")
    groups = lax.axis_size("half") * n_row
    my_child = lax.axis_index("half")
    my_group = my_child * n_row + lax.axis_index("row")
    my_col = lax.axis_index("col")
    cap_cols = 2 * child_cols // n_col
    cap_rows = n_col // n_row * (child_cols // groups + child_cols // n_col)
    slab_rows = n_row * cap_rows
    row_send, row_table = row_tables(row_maps, row_loc, groups, cap_rows, my_group)
    col_send, col_table = col_tables(row_maps, col_loc, n_col, cap_cols, my_col)
    mine = child_blocks[0]
    moved = col_pack(mine, col_send[my_child], n_col * cap_cols)
    arrived = lax.all_to_all(moved, "col", split_axis=1, concat_axis=1, tiled=True)
    outgoing = row_pack(arrived, row_send, groups * cap_rows)
    landed = lax.all_to_all(
        outgoing, ("half", "row"), split_axis=0, concat_axis=0, tiled=True
    ).reshape(2, slab_rows, n_col * cap_cols)
    row_dest = row_table.reshape(2, slab_rows)
    extra = jnp.zeros_like(parent_front)
    for child in range(2):
        spread = (
            jnp.zeros((slab_rows, col_loc), jnp.float32)
            .at[:, col_table[child]]
            .add(landed[child], mode="drop")
        )
        extra = extra.at[row_dest[child]].add(spread, mode="drop")
    assembled = parent_front + extra
    width = inverse_blocks.shape[1]
    count = inverse_blocks.shape[0]
    span = n_col // groups
    root = my_col // span
    start = my_col % span * col_loc
    factors = []
    tops = []
    for block in range(count):
        current = assembled[:, block * width : (block + 1) * width]
        if block > 0:
            earlier = jnp.concatenate(factors, axis=1)
            above = jnp.concatenate(
                [
                    tops[prior][(block - prior - 1) * width : (block - prior) * width]
                    for prior in range(block)
                ],
                axis=1,
            )
            current = current - highest_outer(earlier, above)
        result = highest_outer(current, jnp.tril(inverse_blocks[block]))
        factors.append(result)
        if block + 1 < count:
            tops.append(from_root(result[(block + 1) * width : count * width], ("half", "row"), 0))
    local_factor = jnp.concatenate(factors, axis=1)
    factor_rows = from_root(local_factor, "col", 0)
    piece = lax.dynamic_slice_in_dim(factor_rows, start, col_loc, 0)
    factor_cols = from_root(piece, ("half", "row"), root)
    updated_front = assembled - highest_outer(factor_rows, factor_cols)
    return (updated_front, factor_rows.astype(jnp.bfloat16))


def local(parent_front, child_blocks, row_maps, inverse_blocks):
    col_loc = parent_front.shape[1]
    n_col = lax.axis_size("col")
    n_row = lax.axis_size("row")
    groups = lax.axis_size("half") * n_row
    share = child_blocks.shape[2] // n_col
    panel = inverse_blocks.shape[0] * inverse_blocks.shape[1]
    args = (parent_front, child_blocks, row_maps, inverse_blocks)
    if share % LANES or groups & (groups - 1) or panel > min(parent_front.shape):
        return general(*args)
    plan = column_plan(row_maps, col_loc, n_col, share, panel)
    return lax.cond(plan[-1] <= share, lambda *given: even(*given, plan), general, *args)


def solution(mesh):
    in_specs = (P(("half", "row"), "col"), P("half", "row", "col"), P(), P())
    out_specs = (P(("half", "row"), "col"), P(("half", "row"), None))
    return jax.shard_map(local, mesh=mesh, in_specs=in_specs, out_specs=out_specs, check_vma=False)
```

```python
import functools

import jax
import jax.numpy as jnp
from jax import lax
from jax.experimental import pallas as pl
from jax.experimental.pallas import tpu as pltpu
from jax.sharding import PartitionSpec as P

LANES = 128
CHUNKS = 4
TILE = 256
SLAB = 32
WIDE = 512


def from_root(block, axis, holder):
    block = jnp.where(lax.axis_index(axis) == holder, block, jnp.zeros_like(block))
    return lax.psum(block, axis)


def highest_outer(left, right):
    return lax.dot_general(
        left,
        right,
        (((1,), (1,)), ((), ())),
        precision=lax.Precision.HIGHEST,
        preferred_element_type=jnp.float32,
    )


def ranks(targets, count):
    onehot = (targets[..., None] == jnp.arange(count, dtype=jnp.int32)).astype(jnp.int32)
    before = jnp.cumsum(onehot, axis=-2) - onehot
    return jnp.sum(before * onehot, axis=-1)


def row_tables(row_maps, row_loc, groups, cap_rows, my_group):
    parent_rows = row_maps.reshape(groups, -1)
    targets = parent_rows // row_loc
    slots = ranks(targets, groups)
    sources = jnp.arange(groups, dtype=jnp.int32)[:, None]
    where_at = jnp.where(targets == my_group, sources * cap_rows + slots, groups * cap_rows)
    table = (
        jnp.full((groups * cap_rows,), row_loc, jnp.int32)
        .at[where_at.reshape(-1)]
        .set((parent_rows % row_loc).reshape(-1), mode="drop")
    )
    send_at = targets[my_group] * cap_rows + slots[my_group]
    return (send_at, table)


def col_tables(row_maps, col_loc, n_col, cap_cols, my_col):
    parent_cols = row_maps.reshape(2, n_col, -1)
    targets = parent_cols // col_loc
    slots = ranks(targets, n_col)
    sources = jnp.arange(n_col, dtype=jnp.int32)[None, :, None]
    where_at = jnp.where(targets == my_col, sources * cap_cols + slots, n_col * cap_cols)
    child_index = jnp.broadcast_to(jnp.arange(2, dtype=jnp.int32)[:, None, None], where_at.shape)
    table = (
        jnp.full((2, n_col * cap_cols), col_loc, jnp.int32)
        .at[child_index, where_at]
        .set(parent_cols % col_loc, mode="drop")
    )
    send_at = targets[:, my_col] * cap_cols + slots[:, my_col]
    return (send_at, table)


def row_pack(values, send_at, total):
    return jnp.zeros((total, values.shape[1]), values.dtype).at[send_at].set(values)


def col_pack(values, send_at, total):
    return jnp.zeros((values.shape[0], total), values.dtype).at[:, send_at].set(values)


def round_up(value, step):
    return -(-value // step) * step


def split(values):
    high = lax.reduce_precision(values, 8, 7)
    return high.astype(jnp.bfloat16), (values - high).astype(jnp.bfloat16)


def window_kernel(count, starts, values, *outs):
    size = outs[0].shape[1]
    for way, out in enumerate(outs):
        first = pl.multiple_of(starts[way * count + pl.program_id(0)], 8)
        out[...] = values[:, pl.ds(first, size), :]


def windows(values, starts, size):
    count, length, lanes = values.shape
    ways = starts.shape[0]
    block = lambda rows: pl.BlockSpec((1, rows, lanes), lambda i, *_: (i, 0, 0))
    return pl.pallas_call(
        functools.partial(window_kernel, count),
        grid_spec=pltpu.PrefetchScalarGridSpec(
            num_scalar_prefetch=1, grid=(count,), in_specs=[block(length)], out_specs=[block(size)] * ways
        ),
        out_shape=[jax.ShapeDtypeStruct((count, size, lanes), values.dtype)] * ways,
        cost_estimate=pl.CostEstimate(flops=0, bytes_accessed=8 * ways * count * size * lanes, transcendentals=0),
        name="windows",
    )(starts.reshape(-1), values)


def place_kernel(form, starts, rounds, flags, row_tab, col_tab, base, *refs):
    parts, n_src, n_col, gates, n_landed, update = form
    landed = refs[:n_landed]
    extra = refs[n_landed : n_landed + 2 * update]
    out, spread, rows_high, rows_low = refs[n_landed + 2 * update :]
    tile = pl.program_id(0)
    height, width = base.shape
    window, lanes = landed[0].shape[-2:]
    packed = n_col * lanes
    slab = min(SLAB, window)
    wide = min(WIDE, width)

    def read(source, part, j, rows):
        if len(landed[0].shape) == 5:
            return landed[0][j, source, part, rows, :]
        if n_landed == n_src:
            return landed[source][part, rows, :]
        return landed[part * n_src + source][j, rows, :]

    @pl.when(tile == 0)
    def _():
        column = lax.broadcasted_iota(jnp.int32, (lanes, width), 1)

        def fill(at, carry):
            rows = pl.ds(pl.multiple_of(at * lanes, lanes), lanes)
            spread[rows, :] = (col_tab[rows, :] == column).astype(jnp.bfloat16)
            return carry

        lax.fori_loop(0, 2 * n_col, fill, 0)

    for child in range(2):
        mine = slice(child * packed, (child + 1) * packed)
        rows_high[:, mine] = jnp.zeros((height, packed), jnp.float32)
        rows_low[:, mine] = jnp.zeros((height, packed), jnp.float32)

        def step(turn, carry):
            values, hits = [], []
            for source in range(child * n_src // 2, (child + 1) * n_src // 2):
                for part in range(parts):
                    first = starts[(tile * n_src + source) * parts + part] + turn * slab
                    at = pl.multiple_of(jnp.minimum(first, window - slab), 8)
                    rows = pl.ds(at, slab)
                    values.append(jnp.concatenate([read(source, part, j, rows) for j in range(n_col)], axis=1))
                    index = at + lax.broadcasted_iota(jnp.int32, (slab, height), 0)
                    target = tile * height + lax.broadcasted_iota(jnp.int32, (slab, height), 1)
                    hits.append(((row_tab[source * parts + part, rows, :] == target) & (index >= first)).astype(jnp.float32))
            value = jnp.concatenate(values, axis=0)
            hit = jnp.concatenate(hits, axis=0).astype(jnp.bfloat16)
            high = value.astype(jnp.bfloat16)
            low = (value - high.astype(jnp.float32)).astype(jnp.bfloat16)
            dims = (((0,), (0,)), ((), ()))
            rows_high[:, mine] += lax.dot_general(hit, high, dims, preferred_element_type=jnp.float32)
            rows_low[:, mine] += lax.dot_general(hit, low, dims, preferred_element_type=jnp.float32)
            return carry

        lax.fori_loop(0, rounds[tile * 2 + child], step, 0)

    def matmuls(at, carry):
        cols = pl.ds(pl.multiple_of(at * wide, wide), wide)
        if not gates:
            right = spread[:, cols]
            total = base[:, cols]
            total += jnp.dot(rows_high[...].astype(jnp.bfloat16), right, preferred_element_type=jnp.float32)
            total += jnp.dot(rows_low[...].astype(jnp.bfloat16), right, preferred_element_type=jnp.float32)
            if update:
                left, above = extra
                total += lax.dot_general(
                    left[...], above[cols, :], (((1,), (1,)), ((), ())), preferred_element_type=jnp.float32
                )
            out[:, cols] = total
            return carry
        out[:, cols] = base[:, cols]
        depth = 2 * packed // gates
        for gate in range(gates):

            @pl.when(flags[gate] > 0)
            def _():
                part = slice(gate * depth, (gate + 1) * depth)
                right = spread[part, cols]
                total = jnp.dot(rows_high[:, part].astype(jnp.bfloat16), right, preferred_element_type=jnp.float32)
                total += jnp.dot(rows_low[:, part].astype(jnp.bfloat16), right, preferred_element_type=jnp.float32)
                out[:, cols] += total

        return carry

    lax.fori_loop(0, width // wide, matmuls, 0)


def place(base, landed, row_tab, col_tab, gates=0, factor=None):
    height, width = base.shape
    n_src, parts, window = row_tab.shape
    n_col, lanes = col_tab.shape[1:]
    packed = n_col * lanes
    tile = min(TILE, height)
    tiles = height // tile
    slab = min(SLAB, window)
    edges = jnp.arange(tiles + 1, dtype=jnp.int32) * tile
    inside = row_tab >= 0
    past = jnp.sum((jnp.where(inside, row_tab, height)[..., None, :] < edges[:, None]).astype(jnp.int32), axis=-1)
    ahead = jnp.argmax(inside.astype(jnp.int32), axis=-1)[..., None]
    first = (ahead + past[..., :-1]) // 8 * 8
    last = ahead + past[..., 1:]
    count = jnp.where(past[..., 1:] > past[..., :-1], (last - first + slab - 1) // slab, 0)
    rounds = jnp.max(count.reshape(2, -1, tiles), axis=1)
    flags = jnp.zeros((1,), jnp.int32)
    if gates:
        flags = jnp.any((col_tab >= 0).reshape(gates, -1), axis=1).astype(jnp.int32)
        rounds = rounds * jnp.max(flags.reshape(2, -1), axis=1)[:, None]
    starts = jnp.moveaxis(first, -1, 0).reshape(-1)
    extra = [] if factor is None else list(factor)
    whole = lambda shape: pl.BlockSpec(shape, lambda *_: (0,) * len(shape), pipeline_mode=pl.Buffered(1))
    block = lambda shape: pl.BlockSpec(shape, lambda i, *_: (i, 0))
    spec = pltpu.PrefetchScalarGridSpec(
        num_scalar_prefetch=3,
        grid=(tiles,),
        in_specs=[whole((n_src * parts, window, 1)), whole((2 * packed, 1)), block((tile, width))]
        + [whole(array.shape) for array in landed]
        + ([block((tile, extra[0].shape[1])), whole(extra[1].shape)] if extra else []),
        out_specs=block((tile, width)),
        scratch_shapes=[
            pltpu.VMEM((2 * packed, width), jnp.bfloat16),
            pltpu.VMEM((tile, 2 * packed), jnp.float32),
            pltpu.VMEM((tile, 2 * packed), jnp.float32),
        ],
    )
    return pl.pallas_call(
        functools.partial(place_kernel, (parts, n_src, n_col, gates, len(landed), 1 if extra else 0)),
        grid_spec=spec,
        out_shape=jax.ShapeDtypeStruct(base.shape, base.dtype),
        compiler_params=pltpu.CompilerParams(vmem_limit_bytes=62 * 2**20),
        cost_estimate=pl.CostEstimate(
            flops=8 * height * packed * width, bytes_accessed=8 * height * width + 4 * parts * n_src * packed * window, transcendentals=0
        ),
        name="place",
    )(starts, rounds.T.reshape(-1), flags, row_tab.reshape(n_src * parts, window, 1), col_tab.reshape(-1, 1), base, *landed, *extra)


def earlier_count(marks):
    size = marks.shape[-2]
    before = (jnp.arange(size)[:, None] > jnp.arange(size)[None, :]).astype(jnp.bfloat16)
    counts = jnp.einsum("ab,csbn->csan", before, marks.astype(jnp.bfloat16), preferred_element_type=jnp.float32)
    return counts.astype(jnp.int32)


def column_plan(row_maps, col_loc, n_col, share, panel):
    parent_cols = row_maps.reshape(2, n_col, -1)
    owner = parent_cols // col_loc
    onehot = owner[..., None] == jnp.arange(n_col, dtype=jnp.int32)
    rank = jnp.sum(jnp.where(onehot, earlier_count(onehot), 0), axis=-1)
    over = rank >= share
    early = parent_cols < panel
    marks = jnp.stack([over, early], axis=-1)
    order = earlier_count(marks)
    most = jnp.max(jnp.sum(marks.astype(jnp.int32), axis=2))
    send = jnp.where(over, -1, rank)
    send_over = jnp.where(over, order[..., 0], -1)
    send_early = jnp.where(early, order[..., 1], -1)
    return parent_cols, owner, send, send_over, send_early, most


def seen_from(here, parent_cols, slot, col_loc, count):
    hit = (slot[..., None] == jnp.arange(count, dtype=jnp.int32)) & here[..., None]
    return jnp.sum(jnp.where(hit, parent_cols[..., None] % col_loc + 1, 0), axis=2) - 1


def panel_of(columns, inverses, tops):
    count, width = inverses.shape[:2]
    factors = []
    for block in range(count):
        current = columns[:, block * width : (block + 1) * width]
        if block > 0:
            earlier = jnp.concatenate(factors, axis=1)
            above = (earlier if tops is None else tops)[block * width : (block + 1) * width, : block * width]
            current = current - highest_outer(earlier, above)
        factors.append(highest_outer(current, inverses[block]))
    return jnp.concatenate(factors, axis=1)


def even(parent_front, child_blocks, row_maps, inverse_blocks, plan):
    row_loc, col_loc = parent_front.shape
    child_rows, child_cols = child_blocks.shape[1:]
    n_row, n_col = lax.axis_size("row"), lax.axis_size("col")
    groups = lax.axis_size("half") * n_row
    my_child = lax.axis_index("half")
    my_group = my_child * n_row + lax.axis_index("row")
    my_col = lax.axis_index("col")
    cap_rows = n_col // n_row * (child_cols // groups + child_cols // n_col)
    share = child_cols // n_col
    panel = inverse_blocks.shape[0] * inverse_blocks.shape[1]
    parent_cols, owner, send, send_over, send_early, _ = plan
    pick_at = lambda array, at: lax.dynamic_index_in_dim(array, at, 0, keepdims=False)
    here = owner == my_col
    ordered = lambda tab: jnp.stack([pick_at(tab, my_child), pick_at(tab, 1 - my_child)])
    col_tab = ordered(seen_from(here, parent_cols, send, col_loc, share))
    over_tab = ordered(seen_from(here, parent_cols, send_over, col_loc, share))
    at_col = lambda array: lax.dynamic_slice_in_dim(array, my_col, 1, 1)
    early_cols = at_col(parent_cols)
    early_tab = ordered(seen_from(early_cols >= 0, early_cols, at_col(send_early), panel, share))
    own = lambda array: pick_at(pick_at(array, my_child), my_col)
    slots = jnp.arange(share, dtype=jnp.int32)
    owners = jnp.arange(n_col, dtype=jnp.int32)
    pick = ((own(owner)[:, None, None] == owners[:, None]) & (own(send)[:, None, None] == slots)).astype(jnp.bfloat16)
    pick_first = jnp.stack([own(send_over)[:, None] == slots, own(send_early)[:, None] == slots], axis=1).astype(jnp.bfloat16)

    blocks = row_maps.reshape(groups, child_rows)
    order = jnp.sort(blocks * child_rows + jnp.arange(child_rows, dtype=jnp.int32), axis=1)
    sorted_row = jnp.swapaxes((order // child_rows).reshape(groups, -1, CHUNKS), 1, 2)
    from_row = pick_at(order, my_group) % child_rows
    edges = jnp.arange(groups, dtype=jnp.int32) * row_loc
    begin = jnp.sum((blocks[:, None, :] < edges[:, None]).astype(jnp.int32), axis=-1)
    length = child_rows // CHUNKS
    size = min(round_up(-(-cap_rows // CHUNKS), 8) + 8, length)
    chunks = jnp.arange(CHUNKS, dtype=jnp.int32)
    first = jnp.maximum(begin[..., None] - chunks + CHUNKS - 1, 0) // CHUNKS
    first = jnp.minimum(first // 8 * 8, length - size)
    ways = jnp.bitwise_xor(my_group, jnp.arange(groups, dtype=jnp.int32))
    starts = pick_at(first, my_group)[ways]
    opening = lax.dynamic_index_in_dim(first, my_group, 1, keepdims=False)

    def table(source):
        rows, opens = pick_at(sorted_row, source), pick_at(opening, source)
        return jnp.stack([lax.dynamic_slice_in_dim(rows[chunk], opens[chunk], size, 0) for chunk in range(CHUNKS)])

    row_tab = jnp.stack([table(ways[way]) for way in range(groups)]) - my_group * row_loc
    row_tab = jnp.where((row_tab >= 0) & (row_tab < row_loc), row_tab, -1)

    def row_exchange(pieces):
        swaps = [[(group, group ^ way) for group in range(groups)] for way in range(groups)]
        return [pieces[0]] + [lax.ppermute(pieces[way], ("half", "row"), swaps[way]) for way in range(1, groups)]

    def packed(pair, choice):
        form = "rk,kdu->dru"
        return jnp.einsum(form, pair[0], choice, preferred_element_type=jnp.float32) + jnp.einsum(
            form, pair[1], choice, preferred_element_type=jnp.float32
        )

    mine = child_blocks[0]
    pairs = [split(mine[from_row[chunk::CHUNKS]]) for chunk in range(CHUNKS)]
    ahead = jnp.concatenate([packed(pair, pick_first) for pair in pairs], axis=0)
    ahead = windows(ahead, jnp.repeat(starts, 2, axis=1), size)
    ahead = row_exchange(ahead)
    ahead = [piece.reshape(CHUNKS, 2, size, share) for piece in ahead]
    over = jnp.stack([piece[:, 0] for piece in ahead])
    early = [piece[:, 1] for piece in ahead]

    def column_exchange(chunk, after):
        moved = packed(pairs[chunk], pick)
        if after:
            moved, *_ = lax.optimization_barrier((moved, *after))
        return lax.all_to_all(moved, "col", split_axis=0, concat_axis=0, tiled=True)

    arrived, landed = [], []
    for chunk in range(CHUNKS):
        arrived.append(column_exchange(chunk, landed[-groups:] if chunk > 1 else []))
        if chunk:
            pieces = windows(arrived[chunk - 1], jnp.repeat(starts[:, chunk - 1 : chunk], n_col, axis=1), size)
            landed += row_exchange(pieces)
    pieces = windows(arrived[-1], jnp.repeat(starts[:, CHUNKS - 1 :], n_col, axis=1), size)
    landed += row_exchange(pieces)

    front = parent_front[:, :panel]
    front = jnp.where(my_col == 0, front, jnp.zeros_like(front))
    front, _ = lax.optimization_barrier((front, arrived[0]))
    front = place(front, early, row_tab, early_tab)
    front = lax.psum(front, "col")
    over = lax.all_gather(over, "col", axis=0)
    front, _ = lax.optimization_barrier((front, arrived[-1]))

    corner = front[:panel]
    sent = [lax.ppermute(corner, ("half", "row"), [(0, way)]) for way in range(1, groups)]
    corner = jnp.where(my_group == 0, corner, functools.reduce(jnp.add, sent))
    inverses = jnp.tril(inverse_blocks)
    factor_rows = panel_of(front, inverses, panel_of(corner, inverses, None))
    span = n_col // groups
    piece = lax.dynamic_slice_in_dim(factor_rows, my_col % span * col_loc, col_loc, 0)
    spots = [(col // span * n_col + col, col) for col in range(n_col)]
    sent = [
        lax.ppermute(piece, ("half", "row", "col"), [(at, ((at // n_col) ^ way) * n_col + col) for at, col in spots])
        for way in range(1, groups)
    ]
    factor_cols = jnp.where(my_group == my_col // span, piece, functools.reduce(jnp.add, sent))
    row_high, row_low = split(-factor_rows)
    col_high, col_low = split(factor_cols)
    left = jnp.concatenate([row_high, row_high, row_low], axis=1)
    above = jnp.concatenate([col_high, col_low, col_high], axis=1)

    first_sum = place(parent_front, [over], row_tab, over_tab, gates=4)
    updated = place(first_sum, landed, row_tab, col_tab, factor=(left, above))
    return updated, factor_rows.astype(jnp.bfloat16)


def general(parent_front, child_blocks, row_maps, inverse_blocks):
    row_loc, col_loc = parent_front.shape
    child_rows, child_cols = (child_blocks.shape[1], child_blocks.shape[2])
    n_row = lax.axis_size("row")
    n_col = lax.axis_size("col")
    groups = lax.axis_size("half") * n_row
    my_child = lax.axis_index("half")
    my_group = my_child * n_row + lax.axis_index("row")
    my_col = lax.axis_index("col")
    cap_cols = 2 * child_cols // n_col
    cap_rows = n_col // n_row * (child_cols // groups + child_cols // n_col)
    slab_rows = n_row * cap_rows
    row_send, row_table = row_tables(row_maps, row_loc, groups, cap_rows, my_group)
    col_send, col_table = col_tables(row_maps, col_loc, n_col, cap_cols, my_col)
    mine = child_blocks[0]
    moved = col_pack(mine, col_send[my_child], n_col * cap_cols)
    arrived = lax.all_to_all(moved, "col", split_axis=1, concat_axis=1, tiled=True)
    outgoing = row_pack(arrived, row_send, groups * cap_rows)
    landed = lax.all_to_all(
        outgoing, ("half", "row"), split_axis=0, concat_axis=0, tiled=True
    ).reshape(2, slab_rows, n_col * cap_cols)
    row_dest = row_table.reshape(2, slab_rows)
    extra = jnp.zeros_like(parent_front)
    for child in range(2):
        spread = (
            jnp.zeros((slab_rows, col_loc), jnp.float32)
            .at[:, col_table[child]]
            .add(landed[child], mode="drop")
        )
        extra = extra.at[row_dest[child]].add(spread, mode="drop")
    assembled = parent_front + extra
    width = inverse_blocks.shape[1]
    count = inverse_blocks.shape[0]
    span = n_col // groups
    root = my_col // span
    start = my_col % span * col_loc
    factors = []
    tops = []
    for block in range(count):
        current = assembled[:, block * width : (block + 1) * width]
        if block > 0:
            earlier = jnp.concatenate(factors, axis=1)
            above = jnp.concatenate(
                [
                    tops[prior][(block - prior - 1) * width : (block - prior) * width]
                    for prior in range(block)
                ],
                axis=1,
            )
            current = current - highest_outer(earlier, above)
        result = highest_outer(current, jnp.tril(inverse_blocks[block]))
        factors.append(result)
        if block + 1 < count:
            tops.append(from_root(result[(block + 1) * width : count * width], ("half", "row"), 0))
    local_factor = jnp.concatenate(factors, axis=1)
    factor_rows = from_root(local_factor, "col", 0)
    piece = lax.dynamic_slice_in_dim(factor_rows, start, col_loc, 0)
    factor_cols = from_root(piece, ("half", "row"), root)
    updated_front = assembled - highest_outer(factor_rows, factor_cols)
    return (updated_front, factor_rows.astype(jnp.bfloat16))


def local(parent_front, child_blocks, row_maps, inverse_blocks):
    col_loc = parent_front.shape[1]
    n_col = lax.axis_size("col")
    n_row = lax.axis_size("row")
    groups = lax.axis_size("half") * n_row
    share = child_blocks.shape[2] // n_col
    panel = inverse_blocks.shape[0] * inverse_blocks.shape[1]
    args = (parent_front, child_blocks, row_maps, inverse_blocks)
    if share % LANES or groups & (groups - 1) or panel > min(parent_front.shape):
        return general(*args)
    plan = column_plan(row_maps, col_loc, n_col, share, panel)
    return lax.cond(plan[-1] <= share, lambda *given: even(*given, plan), general, *args)


def solution(mesh):
    in_specs = (P(("half", "row"), "col"), P("half", "row", "col"), P(), P())
    out_specs = (P(("half", "row"), "col"), P(("half", "row"), None))
    return jax.shard_map(local, mesh=mesh, in_specs=in_specs, out_specs=out_specs, check_vma=False)
```

```python
import functools

import jax
import jax.numpy as jnp
from jax import lax
from jax.experimental import pallas as pl
from jax.experimental.pallas import tpu as pltpu
from jax.sharding import PartitionSpec as P

LANES = 128
CHUNKS = 4
TILE = 256
SLAB = 32
WIDE = 512


def from_root(block, axis, holder):
    block = jnp.where(lax.axis_index(axis) == holder, block, jnp.zeros_like(block))
    return lax.psum(block, axis)


def highest_outer(left, right):
    return lax.dot_general(
        left,
        right,
        (((1,), (1,)), ((), ())),
        precision=lax.Precision.HIGHEST,
        preferred_element_type=jnp.float32,
    )


def ranks(targets, count):
    onehot = (targets[..., None] == jnp.arange(count, dtype=jnp.int32)).astype(jnp.int32)
    before = jnp.cumsum(onehot, axis=-2) - onehot
    return jnp.sum(before * onehot, axis=-1)


def row_tables(row_maps, row_loc, groups, cap_rows, my_group):
    parent_rows = row_maps.reshape(groups, -1)
    targets = parent_rows // row_loc
    slots = ranks(targets, groups)
    sources = jnp.arange(groups, dtype=jnp.int32)[:, None]
    where_at = jnp.where(targets == my_group, sources * cap_rows + slots, groups * cap_rows)
    table = (
        jnp.full((groups * cap_rows,), row_loc, jnp.int32)
        .at[where_at.reshape(-1)]
        .set((parent_rows % row_loc).reshape(-1), mode="drop")
    )
    send_at = targets[my_group] * cap_rows + slots[my_group]
    return (send_at, table)


def col_tables(row_maps, col_loc, n_col, cap_cols, my_col):
    parent_cols = row_maps.reshape(2, n_col, -1)
    targets = parent_cols // col_loc
    slots = ranks(targets, n_col)
    sources = jnp.arange(n_col, dtype=jnp.int32)[None, :, None]
    where_at = jnp.where(targets == my_col, sources * cap_cols + slots, n_col * cap_cols)
    child_index = jnp.broadcast_to(jnp.arange(2, dtype=jnp.int32)[:, None, None], where_at.shape)
    table = (
        jnp.full((2, n_col * cap_cols), col_loc, jnp.int32)
        .at[child_index, where_at]
        .set(parent_cols % col_loc, mode="drop")
    )
    send_at = targets[:, my_col] * cap_cols + slots[:, my_col]
    return (send_at, table)


def row_pack(values, send_at, total):
    return jnp.zeros((total, values.shape[1]), values.dtype).at[send_at].set(values)


def col_pack(values, send_at, total):
    return jnp.zeros((values.shape[0], total), values.dtype).at[:, send_at].set(values)


def round_up(value, step):
    return -(-value // step) * step


def split(values):
    high = lax.reduce_precision(values, 8, 7)
    return high.astype(jnp.bfloat16), (values - high).astype(jnp.bfloat16)


def window_kernel(count, starts, values, *outs):
    size = outs[0].shape[1]
    for way, out in enumerate(outs):
        first = pl.multiple_of(starts[way * count + pl.program_id(0)], 8)
        out[...] = values[:, pl.ds(first, size), :]


def windows(values, starts, size):
    count, length, lanes = values.shape
    ways = starts.shape[0]
    block = lambda rows: pl.BlockSpec((1, rows, lanes), lambda i, *_: (i, 0, 0))
    return pl.pallas_call(
        functools.partial(window_kernel, count),
        grid_spec=pltpu.PrefetchScalarGridSpec(
            num_scalar_prefetch=1, grid=(count,), in_specs=[block(length)], out_specs=[block(size)] * ways
        ),
        out_shape=[jax.ShapeDtypeStruct((count, size, lanes), values.dtype)] * ways,
        cost_estimate=pl.CostEstimate(flops=0, bytes_accessed=8 * ways * count * size * lanes, transcendentals=0),
        name="windows",
    )(starts.reshape(-1), values)


def place_kernel(form, starts, rounds, flags, row_tab, col_tab, base, *refs):
    parts, n_src, n_col, gates, n_landed, update = form
    landed = refs[:n_landed]
    extra = refs[n_landed : n_landed + 2 * update]
    out, spread, rows_high, rows_low = refs[n_landed + 2 * update :]
    tile = pl.program_id(0)
    height, width = base.shape
    window, lanes = landed[0].shape[-2:]
    packed = n_col * lanes
    slab = min(SLAB, window)
    wide = min(WIDE, width)

    def read(source, part, j, rows):
        if len(landed[0].shape) == 5:
            near = landed[0].shape[0]
            return landed[j // near][j % near, source, part, rows, :]
        if n_landed == n_src:
            return landed[source][part, rows, :]
        return landed[part * n_src + source][j, rows, :]

    @pl.when(tile == 0)
    def _():
        column = lax.broadcasted_iota(jnp.int32, (lanes, width), 1)

        def fill(at, carry):
            rows = pl.ds(pl.multiple_of(at * lanes, lanes), lanes)
            spread[rows, :] = (col_tab[rows, :] == column).astype(jnp.bfloat16)
            return carry

        lax.fori_loop(0, 2 * n_col, fill, 0)

    for child in range(2):
        mine = slice(child * packed, (child + 1) * packed)
        rows_high[:, mine] = jnp.zeros((height, packed), jnp.float32)
        rows_low[:, mine] = jnp.zeros((height, packed), jnp.float32)

        def step(turn, carry):
            values, hits = [], []
            for source in range(child * n_src // 2, (child + 1) * n_src // 2):
                for part in range(parts):
                    first = starts[(tile * n_src + source) * parts + part] + turn * slab
                    at = pl.multiple_of(jnp.minimum(first, window - slab), 8)
                    rows = pl.ds(at, slab)
                    values.append(jnp.concatenate([read(source, part, j, rows) for j in range(n_col)], axis=1))
                    index = at + lax.broadcasted_iota(jnp.int32, (slab, height), 0)
                    target = tile * height + lax.broadcasted_iota(jnp.int32, (slab, height), 1)
                    hits.append(((row_tab[source * parts + part, rows, :] == target) & (index >= first)).astype(jnp.float32))
            value = jnp.concatenate(values, axis=0)
            hit = jnp.concatenate(hits, axis=0).astype(jnp.bfloat16)
            high = value.astype(jnp.bfloat16)
            low = (value - high.astype(jnp.float32)).astype(jnp.bfloat16)
            dims = (((0,), (0,)), ((), ()))
            rows_high[:, mine] += lax.dot_general(hit, high, dims, preferred_element_type=jnp.float32)
            rows_low[:, mine] += lax.dot_general(hit, low, dims, preferred_element_type=jnp.float32)
            return carry

        lax.fori_loop(0, rounds[tile * 2 + child], step, 0)

    def matmuls(at, carry):
        cols = pl.ds(pl.multiple_of(at * wide, wide), wide)
        if not gates:
            right = spread[:, cols]
            total = base[:, cols]
            total += jnp.dot(rows_high[...].astype(jnp.bfloat16), right, preferred_element_type=jnp.float32)
            total += jnp.dot(rows_low[...].astype(jnp.bfloat16), right, preferred_element_type=jnp.float32)
            if update:
                left, above = extra
                total += lax.dot_general(
                    left[...], above[cols, :], (((1,), (1,)), ((), ())), preferred_element_type=jnp.float32
                )
            out[:, cols] = total
            return carry
        out[:, cols] = base[:, cols]
        depth = 2 * packed // gates
        for gate in range(gates):

            @pl.when(flags[gate] > 0)
            def _():
                part = slice(gate * depth, (gate + 1) * depth)
                right = spread[part, cols]
                total = jnp.dot(rows_high[:, part].astype(jnp.bfloat16), right, preferred_element_type=jnp.float32)
                total += jnp.dot(rows_low[:, part].astype(jnp.bfloat16), right, preferred_element_type=jnp.float32)
                out[:, cols] += total

        return carry

    lax.fori_loop(0, width // wide, matmuls, 0)


def place(base, landed, row_tab, col_tab, gates=0, factor=None):
    height, width = base.shape
    n_src, parts, window = row_tab.shape
    n_col, lanes = col_tab.shape[1:]
    packed = n_col * lanes
    tile = min(TILE, height)
    tiles = height // tile
    slab = min(SLAB, window)
    edges = jnp.arange(tiles + 1, dtype=jnp.int32) * tile
    inside = row_tab >= 0
    past = jnp.sum((jnp.where(inside, row_tab, height)[..., None, :] < edges[:, None]).astype(jnp.int32), axis=-1)
    ahead = jnp.argmax(inside.astype(jnp.int32), axis=-1)[..., None]
    first = (ahead + past[..., :-1]) // 8 * 8
    last = ahead + past[..., 1:]
    count = jnp.where(past[..., 1:] > past[..., :-1], (last - first + slab - 1) // slab, 0)
    rounds = jnp.max(count.reshape(2, -1, tiles), axis=1)
    flags = jnp.zeros((1,), jnp.int32)
    if gates:
        flags = jnp.any((col_tab >= 0).reshape(gates, -1), axis=1).astype(jnp.int32)
        rounds = rounds * jnp.max(flags.reshape(2, -1), axis=1)[:, None]
    starts = jnp.moveaxis(first, -1, 0).reshape(-1)
    extra = [] if factor is None else list(factor)
    whole = lambda shape: pl.BlockSpec(shape, lambda *_: (0,) * len(shape), pipeline_mode=pl.Buffered(1))
    block = lambda shape: pl.BlockSpec(shape, lambda i, *_: (i, 0))
    spec = pltpu.PrefetchScalarGridSpec(
        num_scalar_prefetch=3,
        grid=(tiles,),
        in_specs=[whole((n_src * parts, window, 1)), whole((2 * packed, 1)), block((tile, width))]
        + [whole(array.shape) for array in landed]
        + ([block((tile, extra[0].shape[1])), whole(extra[1].shape)] if extra else []),
        out_specs=block((tile, width)),
        scratch_shapes=[
            pltpu.VMEM((2 * packed, width), jnp.bfloat16),
            pltpu.VMEM((tile, 2 * packed), jnp.float32),
            pltpu.VMEM((tile, 2 * packed), jnp.float32),
        ],
    )
    return pl.pallas_call(
        functools.partial(place_kernel, (parts, n_src, n_col, gates, len(landed), 1 if extra else 0)),
        grid_spec=spec,
        out_shape=jax.ShapeDtypeStruct(base.shape, base.dtype),
        compiler_params=pltpu.CompilerParams(vmem_limit_bytes=62 * 2**20),
        cost_estimate=pl.CostEstimate(
            flops=8 * height * packed * width, bytes_accessed=8 * height * width + 4 * parts * n_src * packed * window, transcendentals=0
        ),
        name="place",
    )(starts, rounds.T.reshape(-1), flags, row_tab.reshape(n_src * parts, window, 1), col_tab.reshape(-1, 1), base, *landed, *extra)


def earlier_count(marks):
    size = marks.shape[-2]
    before = (jnp.arange(size)[:, None] > jnp.arange(size)[None, :]).astype(jnp.bfloat16)
    counts = jnp.einsum("ab,csbn->csan", before, marks.astype(jnp.bfloat16), preferred_element_type=jnp.float32)
    return counts.astype(jnp.int32)


def column_plan(row_maps, col_loc, n_col, share, panel):
    parent_cols = row_maps.reshape(2, n_col, -1)
    owner = parent_cols // col_loc
    onehot = owner[..., None] == jnp.arange(n_col, dtype=jnp.int32)
    rank = jnp.sum(jnp.where(onehot, earlier_count(onehot), 0), axis=-1)
    over = rank >= share
    early = parent_cols < panel
    marks = jnp.stack([over, early], axis=-1)
    order = earlier_count(marks)
    most = jnp.max(jnp.sum(marks.astype(jnp.int32), axis=2))
    send = jnp.where(over, -1, rank)
    send_over = jnp.where(over, order[..., 0], -1)
    send_early = jnp.where(early, order[..., 1], -1)
    return parent_cols, owner, send, send_over, send_early, most


def seen_from(here, parent_cols, slot, col_loc, count):
    hit = (slot[..., None] == jnp.arange(count, dtype=jnp.int32)) & here[..., None]
    return jnp.sum(jnp.where(hit, parent_cols[..., None] % col_loc + 1, 0), axis=2) - 1


def panel_of(columns, inverses, tops):
    count, width = inverses.shape[:2]
    factors = []
    for block in range(count):
        current = columns[:, block * width : (block + 1) * width]
        if block > 0:
            earlier = jnp.concatenate(factors, axis=1)
            above = (earlier if tops is None else tops)[block * width : (block + 1) * width, : block * width]
            current = current - highest_outer(earlier, above)
        factors.append(highest_outer(current, inverses[block]))
    return jnp.concatenate(factors, axis=1)


def even(parent_front, child_blocks, row_maps, inverse_blocks, plan):
    row_loc, col_loc = parent_front.shape
    child_rows, child_cols = child_blocks.shape[1:]
    n_row, n_col = lax.axis_size("row"), lax.axis_size("col")
    groups = lax.axis_size("half") * n_row
    my_child = lax.axis_index("half")
    my_group = my_child * n_row + lax.axis_index("row")
    my_col = lax.axis_index("col")
    cap_rows = n_col // n_row * (child_cols // groups + child_cols // n_col)
    share = child_cols // n_col
    panel = inverse_blocks.shape[0] * inverse_blocks.shape[1]
    parent_cols, owner, send, send_over, send_early, _ = plan
    pick_at = lambda array, at: lax.dynamic_index_in_dim(array, at, 0, keepdims=False)
    here = owner == my_col
    ordered = lambda tab: jnp.stack([pick_at(tab, my_child), pick_at(tab, 1 - my_child)])
    col_tab = ordered(seen_from(here, parent_cols, send, col_loc, share))
    over_tab = ordered(seen_from(here, parent_cols, send_over, col_loc, share))
    at_col = lambda array: lax.dynamic_slice_in_dim(array, my_col, 1, 1)
    early_cols = at_col(parent_cols)
    early_tab = ordered(seen_from(early_cols >= 0, early_cols, at_col(send_early), panel, share))
    own = lambda array: pick_at(pick_at(array, my_child), my_col)
    slots = jnp.arange(share, dtype=jnp.int32)
    owners = jnp.arange(n_col, dtype=jnp.int32)
    pick = ((own(owner)[:, None, None] == owners[:, None]) & (own(send)[:, None, None] == slots)).astype(jnp.bfloat16)
    pick_first = jnp.stack([own(send_over)[:, None] == slots, own(send_early)[:, None] == slots], axis=1).astype(jnp.bfloat16)

    blocks = row_maps.reshape(groups, child_rows)
    order = jnp.sort(blocks * child_rows + jnp.arange(child_rows, dtype=jnp.int32), axis=1)
    sorted_row = jnp.swapaxes((order // child_rows).reshape(groups, -1, CHUNKS), 1, 2)
    from_row = pick_at(order, my_group) % child_rows
    edges = jnp.arange(groups, dtype=jnp.int32) * row_loc
    begin = jnp.sum((blocks[:, None, :] < edges[:, None]).astype(jnp.int32), axis=-1)
    length = child_rows // CHUNKS
    size = min(round_up(-(-cap_rows // CHUNKS), 8) + 8, length)
    chunks = jnp.arange(CHUNKS, dtype=jnp.int32)
    first = jnp.maximum(begin[..., None] - chunks + CHUNKS - 1, 0) // CHUNKS
    first = jnp.minimum(first // 8 * 8, length - size)
    ways = jnp.bitwise_xor(my_group, jnp.arange(groups, dtype=jnp.int32))
    starts = pick_at(first, my_group)[ways]
    opening = lax.dynamic_index_in_dim(first, my_group, 1, keepdims=False)

    def table(source):
        rows, opens = pick_at(sorted_row, source), pick_at(opening, source)
        return jnp.stack([lax.dynamic_slice_in_dim(rows[chunk], opens[chunk], size, 0) for chunk in range(CHUNKS)])

    row_tab = jnp.stack([table(ways[way]) for way in range(groups)]) - my_group * row_loc
    row_tab = jnp.where((row_tab >= 0) & (row_tab < row_loc), row_tab, -1)

    def row_exchange(pieces):
        swaps = [[(group, group ^ way) for group in range(groups)] for way in range(groups)]
        return [pieces[0]] + [lax.ppermute(pieces[way], ("half", "row"), swaps[way]) for way in range(1, groups)]

    def packed(pair, choice):
        form = "rk,kdu->dru"
        return jnp.einsum(form, pair[0], choice, preferred_element_type=jnp.float32) + jnp.einsum(
            form, pair[1], choice, preferred_element_type=jnp.float32
        )

    mine = child_blocks[0]
    pairs = [split(mine[from_row[chunk::CHUNKS]]) for chunk in range(CHUNKS)]
    ahead = jnp.concatenate([packed(pair, pick_first) for pair in pairs], axis=0)
    ahead = windows(ahead, jnp.repeat(starts, 2, axis=1), size)
    ahead = row_exchange(ahead)
    ahead = [piece.reshape(CHUNKS, 2, size, share) for piece in ahead]
    over = jnp.stack([piece[:, 0] for piece in ahead])
    early = [piece[:, 1] for piece in ahead]

    def column_exchange(chunk, after):
        moved = packed(pairs[chunk], pick)
        if after:
            moved, *_ = lax.optimization_barrier((moved, *after))
        return lax.all_to_all(moved, "col", split_axis=0, concat_axis=0, tiled=True)

    staged = n_col == 8
    if staged:
        deep, side = my_col // 2, my_col % 2
        far = jnp.where(deep < 2, jnp.array([2, 3]), jnp.array([1, 0]))
        near = jnp.stack([deep, jnp.bitwise_xor(deep, 1)])
        sides = jnp.stack([side, 1 - side])
        origin = jnp.stack([near[None] * 2 + sides[:, None], far[None] * 2 + sides[:, None]]).reshape(-1)
        over_tab = over_tab[:, origin]
        along = lambda pairs: [(z * 2 + y, to * 2 + y) for z, to in pairs for y in range(2)]
        across = [(col, col ^ 1) for col in range(n_col)]
        swapped = lax.ppermute(over, "col", along([(z, z ^ 1) for z in range(4)]))
        near_over = jnp.stack([over, swapped])
        middle = lax.ppermute(near_over, "col", along([(1, 2), (2, 1)]))
        near_side = lax.ppermute(near_over, "col", across)
        outward = lax.ppermute(middle, "col", along([(1, 0), (2, 3)]))
        far_over = middle + outward
        far_side = lax.ppermute(far_over, "col", across)
        over = [near_over, near_side, far_over, far_side]
        before_exchange = [[], [near_over], [], []]
        before_windows = [[], [middle, near_side], [outward], []]
    else:
        over = [lax.all_gather(over, "col", axis=0)]
        before_exchange = before_windows = [[]] * 4

    arrived, landed, pieces = [], [], []
    for chunk in range(CHUNKS):
        arrived.append(column_exchange(chunk, list(pieces) + before_exchange[chunk % 4]))
        after = landed[-groups:] + before_windows[chunk % 4]
        value = lax.optimization_barrier((arrived[chunk], *after))[0] if after else arrived[chunk]
        pieces = windows(value, jnp.repeat(starts[:, chunk : chunk + 1], n_col, axis=1), size)
        landed += row_exchange(pieces)

    front = parent_front[:, :panel]
    front = jnp.where(my_col == 0, front, jnp.zeros_like(front))
    front, _ = lax.optimization_barrier((front, arrived[0]))
    front = place(front, early, row_tab, early_tab)
    front = lax.psum(front, "col")
    front, _ = lax.optimization_barrier((front, arrived[-1]))

    corner = front[:panel]
    sent = [lax.ppermute(corner, ("half", "row"), [(0, way)]) for way in range(1, groups)]
    corner = jnp.where(my_group == 0, corner, functools.reduce(jnp.add, sent))
    inverses = jnp.tril(inverse_blocks)
    factor_rows = panel_of(front, inverses, panel_of(corner, inverses, None))
    span = n_col // groups
    piece = lax.dynamic_slice_in_dim(factor_rows, my_col % span * col_loc, col_loc, 0)
    spots = [(col // span * n_col + col, col) for col in range(n_col)]
    sent = [
        lax.ppermute(piece, ("half", "row", "col"), [(at, ((at // n_col) ^ way) * n_col + col) for at, col in spots])
        for way in range(1, groups)
    ]
    factor_cols = jnp.where(my_group == my_col // span, piece, functools.reduce(jnp.add, sent))
    row_high, row_low = split(-factor_rows)
    col_high, col_low = split(factor_cols)
    left = jnp.concatenate([row_high, row_high, row_low], axis=1)
    above = jnp.concatenate([col_high, col_low, col_high], axis=1)

    first_sum = place(parent_front, over, row_tab, over_tab, gates=4)
    updated = place(first_sum, landed, row_tab, col_tab, factor=(left, above))
    return updated, factor_rows.astype(jnp.bfloat16)


def general(parent_front, child_blocks, row_maps, inverse_blocks):
    row_loc, col_loc = parent_front.shape
    child_rows, child_cols = (child_blocks.shape[1], child_blocks.shape[2])
    n_row = lax.axis_size("row")
    n_col = lax.axis_size("col")
    groups = lax.axis_size("half") * n_row
    my_child = lax.axis_index("half")
    my_group = my_child * n_row + lax.axis_index("row")
    my_col = lax.axis_index("col")
    cap_cols = 2 * child_cols // n_col
    cap_rows = n_col // n_row * (child_cols // groups + child_cols // n_col)
    slab_rows = n_row * cap_rows
    row_send, row_table = row_tables(row_maps, row_loc, groups, cap_rows, my_group)
    col_send, col_table = col_tables(row_maps, col_loc, n_col, cap_cols, my_col)
    mine = child_blocks[0]
    moved = col_pack(mine, col_send[my_child], n_col * cap_cols)
    arrived = lax.all_to_all(moved, "col", split_axis=1, concat_axis=1, tiled=True)
    outgoing = row_pack(arrived, row_send, groups * cap_rows)
    landed = lax.all_to_all(
        outgoing, ("half", "row"), split_axis=0, concat_axis=0, tiled=True
    ).reshape(2, slab_rows, n_col * cap_cols)
    row_dest = row_table.reshape(2, slab_rows)
    extra = jnp.zeros_like(parent_front)
    for child in range(2):
        spread = (
            jnp.zeros((slab_rows, col_loc), jnp.float32)
            .at[:, col_table[child]]
            .add(landed[child], mode="drop")
        )
        extra = extra.at[row_dest[child]].add(spread, mode="drop")
    assembled = parent_front + extra
    width = inverse_blocks.shape[1]
    count = inverse_blocks.shape[0]
    span = n_col // groups
    root = my_col // span
    start = my_col % span * col_loc
    factors = []
    tops = []
    for block in range(count):
        current = assembled[:, block * width : (block + 1) * width]
        if block > 0:
            earlier = jnp.concatenate(factors, axis=1)
            above = jnp.concatenate(
                [
                    tops[prior][(block - prior - 1) * width : (block - prior) * width]
                    for prior in range(block)
                ],
                axis=1,
            )
            current = current - highest_outer(earlier, above)
        result = highest_outer(current, jnp.tril(inverse_blocks[block]))
        factors.append(result)
        if block + 1 < count:
            tops.append(from_root(result[(block + 1) * width : count * width], ("half", "row"), 0))
    local_factor = jnp.concatenate(factors, axis=1)
    factor_rows = from_root(local_factor, "col", 0)
    piece = lax.dynamic_slice_in_dim(factor_rows, start, col_loc, 0)
    factor_cols = from_root(piece, ("half", "row"), root)
    updated_front = assembled - highest_outer(factor_rows, factor_cols)
    return (updated_front, factor_rows.astype(jnp.bfloat16))


def local(parent_front, child_blocks, row_maps, inverse_blocks):
    col_loc = parent_front.shape[1]
    n_col = lax.axis_size("col")
    n_row = lax.axis_size("row")
    groups = lax.axis_size("half") * n_row
    share = child_blocks.shape[2] // n_col
    panel = inverse_blocks.shape[0] * inverse_blocks.shape[1]
    args = (parent_front, child_blocks, row_maps, inverse_blocks)
    if share % LANES or groups & (groups - 1) or panel > min(parent_front.shape):
        return general(*args)
    plan = column_plan(row_maps, col_loc, n_col, share, panel)
    return lax.cond(plan[-1] <= share, lambda *given: even(*given, plan), general, *args)


def solution(mesh):
    in_specs = (P(("half", "row"), "col"), P("half", "row", "col"), P(), P())
    out_specs = (P(("half", "row"), "col"), P(("half", "row"), None))
    return jax.shard_map(local, mesh=mesh, in_specs=in_specs, out_specs=out_specs, check_vma=False)
```

```python
import functools

import jax
import jax.numpy as jnp
from jax import lax
from jax.experimental import pallas as pl
from jax.experimental.pallas import tpu as pltpu
from jax.sharding import PartitionSpec as P

LANES = 128
CHUNKS = 4
TILE = 256
SLAB = 32
WIDE = 512


def from_root(block, axis, holder):
    block = jnp.where(lax.axis_index(axis) == holder, block, jnp.zeros_like(block))
    return lax.psum(block, axis)


def highest_outer(left, right):
    return lax.dot_general(
        left,
        right,
        (((1,), (1,)), ((), ())),
        precision=lax.Precision.HIGHEST,
        preferred_element_type=jnp.float32,
    )


def ranks(targets, count):
    onehot = (targets[..., None] == jnp.arange(count, dtype=jnp.int32)).astype(jnp.int32)
    before = jnp.cumsum(onehot, axis=-2) - onehot
    return jnp.sum(before * onehot, axis=-1)


def row_tables(row_maps, row_loc, groups, cap_rows, my_group):
    parent_rows = row_maps.reshape(groups, -1)
    targets = parent_rows // row_loc
    slots = ranks(targets, groups)
    sources = jnp.arange(groups, dtype=jnp.int32)[:, None]
    where_at = jnp.where(targets == my_group, sources * cap_rows + slots, groups * cap_rows)
    table = (
        jnp.full((groups * cap_rows,), row_loc, jnp.int32)
        .at[where_at.reshape(-1)]
        .set((parent_rows % row_loc).reshape(-1), mode="drop")
    )
    send_at = targets[my_group] * cap_rows + slots[my_group]
    return (send_at, table)


def col_tables(row_maps, col_loc, n_col, cap_cols, my_col):
    parent_cols = row_maps.reshape(2, n_col, -1)
    targets = parent_cols // col_loc
    slots = ranks(targets, n_col)
    sources = jnp.arange(n_col, dtype=jnp.int32)[None, :, None]
    where_at = jnp.where(targets == my_col, sources * cap_cols + slots, n_col * cap_cols)
    child_index = jnp.broadcast_to(jnp.arange(2, dtype=jnp.int32)[:, None, None], where_at.shape)
    table = (
        jnp.full((2, n_col * cap_cols), col_loc, jnp.int32)
        .at[child_index, where_at]
        .set(parent_cols % col_loc, mode="drop")
    )
    send_at = targets[:, my_col] * cap_cols + slots[:, my_col]
    return (send_at, table)


def row_pack(values, send_at, total):
    return jnp.zeros((total, values.shape[1]), values.dtype).at[send_at].set(values)


def col_pack(values, send_at, total):
    return jnp.zeros((values.shape[0], total), values.dtype).at[:, send_at].set(values)


def round_up(value, step):
    return -(-value // step) * step


def split(values):
    high = lax.reduce_precision(values, 8, 7)
    return high.astype(jnp.bfloat16), (values - high).astype(jnp.bfloat16)


def window_kernel(count, starts, values, *outs):
    size = outs[0].shape[1]
    for way, out in enumerate(outs):
        first = pl.multiple_of(starts[way * count + pl.program_id(0)], 8)
        out[...] = values[:, pl.ds(first, size), :]


def windows(values, starts, size):
    count, length, lanes = values.shape
    ways = starts.shape[0]
    block = lambda rows: pl.BlockSpec((1, rows, lanes), lambda i, *_: (i, 0, 0))
    return pl.pallas_call(
        functools.partial(window_kernel, count),
        grid_spec=pltpu.PrefetchScalarGridSpec(
            num_scalar_prefetch=1, grid=(count,), in_specs=[block(length)], out_specs=[block(size)] * ways
        ),
        out_shape=[jax.ShapeDtypeStruct((count, size, lanes), values.dtype)] * ways,
        cost_estimate=pl.CostEstimate(flops=0, bytes_accessed=8 * ways * count * size * lanes, transcendentals=0),
        name="windows",
    )(starts.reshape(-1), values)


def place_kernel(form, starts, rounds, flags, row_tab, col_tab, base, *refs):
    parts, n_src, n_col, gates, n_landed, update = form
    landed = refs[:n_landed]
    extra = refs[n_landed : n_landed + 2 * update]
    out, spread, rows_high, rows_low = refs[n_landed + 2 * update :]
    tile = pl.program_id(0)
    height, width = base.shape
    window, lanes = landed[0].shape[-2:]
    packed = n_col * lanes
    slab = min(SLAB, window)
    wide = min(WIDE, width)

    def read(source, part, j, rows):
        if len(landed[0].shape) == 5:
            near = landed[0].shape[0]
            return landed[j // near][j % near, source, part, rows, :]
        if n_landed == n_src:
            return landed[source][part, rows, :]
        return landed[part * n_src + source][j, rows, :]

    @pl.when(tile == 0)
    def _():
        column = lax.broadcasted_iota(jnp.int32, (lanes, width), 1)

        def fill(at, carry):
            rows = pl.ds(pl.multiple_of(at * lanes, lanes), lanes)
            spread[rows, :] = (col_tab[rows, :] == column).astype(jnp.bfloat16)
            return carry

        lax.fori_loop(0, 2 * n_col, fill, 0)

    for child in range(2):
        mine = slice(child * packed, (child + 1) * packed)
        rows_high[:, mine] = jnp.zeros((height, packed), jnp.float32)
        rows_low[:, mine] = jnp.zeros((height, packed), jnp.float32)

        def step(turn, carry):
            values, hits = [], []
            for source in range(child * n_src // 2, (child + 1) * n_src // 2):
                for part in range(parts):
                    first = starts[(tile * n_src + source) * parts + part] + turn * slab
                    at = pl.multiple_of(jnp.minimum(first, window - slab), 8)
                    rows = pl.ds(at, slab)
                    values.append(jnp.concatenate([read(source, part, j, rows) for j in range(n_col)], axis=1))
                    index = at + lax.broadcasted_iota(jnp.int32, (slab, height), 0)
                    target = tile * height + lax.broadcasted_iota(jnp.int32, (slab, height), 1)
                    hits.append(((row_tab[source * parts + part, rows, :] == target) & (index >= first)).astype(jnp.float32))
            value = jnp.concatenate(values, axis=0)
            hit = jnp.concatenate(hits, axis=0).astype(jnp.bfloat16)
            high = value.astype(jnp.bfloat16)
            low = (value - high.astype(jnp.float32)).astype(jnp.bfloat16)
            dims = (((0,), (0,)), ((), ()))
            rows_high[:, mine] += lax.dot_general(hit, high, dims, preferred_element_type=jnp.float32)
            rows_low[:, mine] += lax.dot_general(hit, low, dims, preferred_element_type=jnp.float32)
            return carry

        lax.fori_loop(0, rounds[tile * 2 + child], step, 0)

    def matmuls(at, carry):
        cols = pl.ds(pl.multiple_of(at * wide, wide), wide)
        if not gates:
            right = spread[:, cols]
            total = base[:, cols]
            total += jnp.dot(rows_high[...].astype(jnp.bfloat16), right, preferred_element_type=jnp.float32)
            total += jnp.dot(rows_low[...].astype(jnp.bfloat16), right, preferred_element_type=jnp.float32)
            if update:
                left, above = extra
                total += lax.dot_general(
                    left[...], above[cols, :], (((1,), (1,)), ((), ())), preferred_element_type=jnp.float32
                )
            out[:, cols] = total
            return carry
        out[:, cols] = base[:, cols]
        depth = 2 * packed // gates
        for gate in range(gates):

            @pl.when(flags[gate] > 0)
            def _():
                part = slice(gate * depth, (gate + 1) * depth)
                right = spread[part, cols]
                total = jnp.dot(rows_high[:, part].astype(jnp.bfloat16), right, preferred_element_type=jnp.float32)
                total += jnp.dot(rows_low[:, part].astype(jnp.bfloat16), right, preferred_element_type=jnp.float32)
                out[:, cols] += total

        return carry

    lax.fori_loop(0, width // wide, matmuls, 0)


def place(base, landed, row_tab, col_tab, gates=0, factor=None):
    height, width = base.shape
    n_src, parts, window = row_tab.shape
    n_col, lanes = col_tab.shape[1:]
    packed = n_col * lanes
    tile = min(TILE, height)
    tiles = height // tile
    slab = min(SLAB, window)
    edges = jnp.arange(tiles + 1, dtype=jnp.int32) * tile
    inside = row_tab >= 0
    past = jnp.sum((jnp.where(inside, row_tab, height)[..., None, :] < edges[:, None]).astype(jnp.int32), axis=-1)
    ahead = jnp.argmax(inside.astype(jnp.int32), axis=-1)[..., None]
    first = (ahead + past[..., :-1]) // 8 * 8
    last = ahead + past[..., 1:]
    count = jnp.where(past[..., 1:] > past[..., :-1], (last - first + slab - 1) // slab, 0)
    rounds = jnp.max(count.reshape(2, -1, tiles), axis=1)
    flags = jnp.zeros((1,), jnp.int32)
    if gates:
        flags = jnp.any((col_tab >= 0).reshape(gates, -1), axis=1).astype(jnp.int32)
        rounds = rounds * jnp.max(flags.reshape(2, -1), axis=1)[:, None]
    starts = jnp.moveaxis(first, -1, 0).reshape(-1)
    extra = [] if factor is None else list(factor)
    whole = lambda shape: pl.BlockSpec(shape, lambda *_: (0,) * len(shape), pipeline_mode=pl.Buffered(1))
    block = lambda shape: pl.BlockSpec(shape, lambda i, *_: (i, 0))
    spec = pltpu.PrefetchScalarGridSpec(
        num_scalar_prefetch=3,
        grid=(tiles,),
        in_specs=[whole((n_src * parts, window, 1)), whole((2 * packed, 1)), block((tile, width))]
        + [whole(array.shape) for array in landed]
        + ([block((tile, extra[0].shape[1])), whole(extra[1].shape)] if extra else []),
        out_specs=block((tile, width)),
        scratch_shapes=[
            pltpu.VMEM((2 * packed, width), jnp.bfloat16),
            pltpu.VMEM((tile, 2 * packed), jnp.float32),
            pltpu.VMEM((tile, 2 * packed), jnp.float32),
        ],
    )
    return pl.pallas_call(
        functools.partial(place_kernel, (parts, n_src, n_col, gates, len(landed), 1 if extra else 0)),
        grid_spec=spec,
        out_shape=jax.ShapeDtypeStruct(base.shape, base.dtype),
        compiler_params=pltpu.CompilerParams(vmem_limit_bytes=62 * 2**20),
        cost_estimate=pl.CostEstimate(
            flops=8 * height * packed * width, bytes_accessed=8 * height * width + 4 * parts * n_src * packed * window, transcendentals=0
        ),
        name="place",
    )(starts, rounds.T.reshape(-1), flags, row_tab.reshape(n_src * parts, window, 1), col_tab.reshape(-1, 1), base, *landed, *extra)


def earlier_count(marks):
    size = marks.shape[-2]
    before = (jnp.arange(size)[:, None] > jnp.arange(size)[None, :]).astype(jnp.bfloat16)
    counts = jnp.einsum("ab,csbn->csan", before, marks.astype(jnp.bfloat16), preferred_element_type=jnp.float32)
    return counts.astype(jnp.int32)


def column_plan(row_maps, col_loc, n_col, share, panel):
    parent_cols = row_maps.reshape(2, n_col, -1)
    owner = parent_cols // col_loc
    onehot = owner[..., None] == jnp.arange(n_col, dtype=jnp.int32)
    rank = jnp.sum(jnp.where(onehot, earlier_count(onehot), 0), axis=-1)
    over = rank >= share
    early = parent_cols < panel
    marks = jnp.stack([over, early], axis=-1)
    order = earlier_count(marks)
    most = jnp.max(jnp.sum(marks.astype(jnp.int32), axis=2))
    send = jnp.where(over, -1, rank)
    send_over = jnp.where(over, order[..., 0], -1)
    send_early = jnp.where(early, order[..., 1], -1)
    return parent_cols, owner, send, send_over, send_early, most


def seen_from(here, parent_cols, slot, col_loc, count):
    hit = (slot[..., None] == jnp.arange(count, dtype=jnp.int32)) & here[..., None]
    return jnp.sum(jnp.where(hit, parent_cols[..., None] % col_loc + 1, 0), axis=2) - 1


def panel_of(columns, inverses, tops):
    count, width = inverses.shape[:2]
    factors = []
    for block in range(count):
        current = columns[:, block * width : (block + 1) * width]
        if block > 0:
            earlier = jnp.concatenate(factors, axis=1)
            above = (earlier if tops is None else tops)[block * width : (block + 1) * width, : block * width]
            current = current - highest_outer(earlier, above)
        factors.append(highest_outer(current, inverses[block]))
    return jnp.concatenate(factors, axis=1)


def even(parent_front, child_blocks, row_maps, inverse_blocks, plan):
    row_loc, col_loc = parent_front.shape
    child_rows, child_cols = child_blocks.shape[1:]
    n_row, n_col = lax.axis_size("row"), lax.axis_size("col")
    groups = lax.axis_size("half") * n_row
    my_child = lax.axis_index("half")
    my_group = my_child * n_row + lax.axis_index("row")
    my_col = lax.axis_index("col")
    cap_rows = n_col // n_row * (child_cols // groups + child_cols // n_col)
    share = child_cols // n_col
    panel = inverse_blocks.shape[0] * inverse_blocks.shape[1]
    parent_cols, owner, send, send_over, send_early, _ = plan
    pick_at = lambda array, at: lax.dynamic_index_in_dim(array, at, 0, keepdims=False)
    here = owner == my_col
    ordered = lambda tab: jnp.stack([pick_at(tab, my_child), pick_at(tab, 1 - my_child)])
    col_tab = ordered(seen_from(here, parent_cols, send, col_loc, share))
    over_tab = ordered(seen_from(here, parent_cols, send_over, col_loc, share))
    at_col = lambda array: lax.dynamic_slice_in_dim(array, my_col, 1, 1)
    early_cols = at_col(parent_cols)
    early_tab = ordered(seen_from(early_cols >= 0, early_cols, at_col(send_early), panel, share))
    own = lambda array: pick_at(pick_at(array, my_child), my_col)
    slots = jnp.arange(share, dtype=jnp.int32)
    owners = jnp.arange(n_col, dtype=jnp.int32)
    pick = ((own(owner)[:, None, None] == owners[:, None]) & (own(send)[:, None, None] == slots)).astype(jnp.bfloat16)
    pick_first = jnp.stack([own(send_over)[:, None] == slots, own(send_early)[:, None] == slots], axis=1).astype(jnp.bfloat16)

    blocks = row_maps.reshape(groups, child_rows)
    order = jnp.sort(blocks * child_rows + jnp.arange(child_rows, dtype=jnp.int32), axis=1)
    sorted_row = jnp.swapaxes((order // child_rows).reshape(groups, -1, CHUNKS), 1, 2)
    from_row = pick_at(order, my_group) % child_rows
    edges = jnp.arange(groups, dtype=jnp.int32) * row_loc
    begin = jnp.sum((blocks[:, None, :] < edges[:, None]).astype(jnp.int32), axis=-1)
    length = child_rows // CHUNKS
    size = min(round_up(-(-cap_rows // CHUNKS), 8) + 8, length)
    chunks = jnp.arange(CHUNKS, dtype=jnp.int32)
    first = jnp.maximum(begin[..., None] - chunks + CHUNKS - 1, 0) // CHUNKS
    first = jnp.minimum(first // 8 * 8, length - size)
    ways = jnp.bitwise_xor(my_group, jnp.arange(groups, dtype=jnp.int32))
    starts = pick_at(first, my_group)[ways]
    opening = lax.dynamic_index_in_dim(first, my_group, 1, keepdims=False)

    def table(source):
        rows, opens = pick_at(sorted_row, source), pick_at(opening, source)
        return jnp.stack([lax.dynamic_slice_in_dim(rows[chunk], opens[chunk], size, 0) for chunk in range(CHUNKS)])

    row_tab = jnp.stack([table(ways[way]) for way in range(groups)]) - my_group * row_loc
    row_tab = jnp.where((row_tab >= 0) & (row_tab < row_loc), row_tab, -1)

    def row_exchange(pieces):
        swaps = [[(group, group ^ way) for group in range(groups)] for way in range(groups)]
        return [pieces[0]] + [lax.ppermute(pieces[way], ("half", "row"), swaps[way]) for way in range(1, groups)]

    def packed(pair, choice):
        form = "rk,kdu->dru"
        return jnp.einsum(form, pair[0], choice, preferred_element_type=jnp.float32) + jnp.einsum(
            form, pair[1], choice, preferred_element_type=jnp.float32
        )

    mine = child_blocks[0]
    pairs = [split(mine[from_row[chunk::CHUNKS]]) for chunk in range(CHUNKS)]
    ahead = jnp.concatenate([packed(pair, pick_first) for pair in pairs], axis=0)
    ahead = windows(ahead, jnp.repeat(starts, 2, axis=1), size)
    ahead = row_exchange(ahead)
    ahead = [piece.reshape(CHUNKS, 2, size, share) for piece in ahead]
    over = jnp.stack([piece[:, 0] for piece in ahead])
    early = [piece[:, 1] for piece in ahead]

    def column_exchange(chunk, after):
        moved = packed(pairs[chunk], pick)
        if after:
            moved, *_ = lax.optimization_barrier((moved, *after))
        return lax.all_to_all(moved, "col", split_axis=0, concat_axis=0, tiled=True)

    staged = n_col == 8
    if staged:
        deep, side = my_col // 2, my_col % 2
        far = jnp.where(deep < 2, jnp.array([2, 3]), jnp.array([1, 0]))
        near = jnp.stack([deep, jnp.bitwise_xor(deep, 1)])
        sides = jnp.stack([side, 1 - side])
        origin = jnp.stack([near[None] * 2 + sides[:, None], far[None] * 2 + sides[:, None]]).reshape(-1)
        over_tab = over_tab[:, origin]
        along = lambda pairs: [(z * 2 + y, to * 2 + y) for z, to in pairs for y in range(2)]
        across = [(col, col ^ 1) for col in range(n_col)]
        swapped = lax.ppermute(over, "col", along([(z, z ^ 1) for z in range(4)]))
        near_over = jnp.stack([over, swapped])
        middle = lax.ppermute(near_over, "col", along([(1, 2), (2, 1)]))
        near_side = lax.ppermute(near_over, "col", across)
        outward = lax.ppermute(middle, "col", along([(1, 0), (2, 3)]))
        far_over = middle + outward
        far_side = lax.ppermute(far_over, "col", across)
        over = [near_over, near_side, far_over, far_side]
        before_exchange = [[], [near_over], [], []]
        before_windows = [[], [middle, near_side], [outward], []]
    else:
        over = [lax.all_gather(over, "col", axis=0)]
        before_exchange, before_windows = [[]] * 4, [[]] * 4

    arrived, landed, pieces = [column_exchange(0, [])], [], []
    front = parent_front[:, :panel]
    front = jnp.where(my_col == 0, front, jnp.zeros_like(front))
    front, _ = lax.optimization_barrier((front, arrived[0]))
    front = place(front, early, row_tab, early_tab)
    before_exchange[1] = before_exchange[1] + [front]
    for chunk in range(CHUNKS):
        if chunk:
            arrived.append(column_exchange(chunk, list(pieces) + before_exchange[chunk % 4]))
        after = landed[-groups:] + before_windows[chunk % 4]
        value = lax.optimization_barrier((arrived[chunk], *after))[0] if after else arrived[chunk]
        pieces = windows(value, jnp.repeat(starts[:, chunk : chunk + 1], n_col, axis=1), size)
        landed += row_exchange(pieces)

    front = lax.psum(front, "col")
    front, _ = lax.optimization_barrier((front, arrived[-2]))

    corner = front[:panel]
    sent = [lax.ppermute(corner, ("half", "row"), [(0, way)]) for way in range(1, groups)]
    corner = jnp.where(my_group == 0, corner, functools.reduce(jnp.add, sent))
    inverses = jnp.tril(inverse_blocks)
    factor_rows = panel_of(front, inverses, panel_of(corner, inverses, None))
    span = n_col // groups
    piece = lax.dynamic_slice_in_dim(factor_rows, my_col % span * col_loc, col_loc, 0)
    spots = [(col // span * n_col + col, col) for col in range(n_col)]
    sent = [
        lax.ppermute(piece, ("half", "row", "col"), [(at, ((at // n_col) ^ way) * n_col + col) for at, col in spots])
        for way in range(1, groups)
    ]
    factor_cols = jnp.where(my_group == my_col // span, piece, functools.reduce(jnp.add, sent))
    row_high, row_low = split(-factor_rows)
    col_high, col_low = split(factor_cols)
    left = jnp.concatenate([row_high, row_high, row_low], axis=1)
    above = jnp.concatenate([col_high, col_low, col_high], axis=1)

    over_tab, *_ = lax.optimization_barrier((over_tab, factor_rows, pieces[0]))
    first_sum = place(parent_front, over, row_tab, over_tab, gates=4)
    updated = place(first_sum, landed, row_tab, col_tab, factor=(left, above))
    return updated, factor_rows.astype(jnp.bfloat16)


def general(parent_front, child_blocks, row_maps, inverse_blocks):
    row_loc, col_loc = parent_front.shape
    child_rows, child_cols = (child_blocks.shape[1], child_blocks.shape[2])
    n_row = lax.axis_size("row")
    n_col = lax.axis_size("col")
    groups = lax.axis_size("half") * n_row
    my_child = lax.axis_index("half")
    my_group = my_child * n_row + lax.axis_index("row")
    my_col = lax.axis_index("col")
    cap_cols = 2 * child_cols // n_col
    cap_rows = n_col // n_row * (child_cols // groups + child_cols // n_col)
    slab_rows = n_row * cap_rows
    row_send, row_table = row_tables(row_maps, row_loc, groups, cap_rows, my_group)
    col_send, col_table = col_tables(row_maps, col_loc, n_col, cap_cols, my_col)
    mine = child_blocks[0]
    moved = col_pack(mine, col_send[my_child], n_col * cap_cols)
    arrived = lax.all_to_all(moved, "col", split_axis=1, concat_axis=1, tiled=True)
    outgoing = row_pack(arrived, row_send, groups * cap_rows)
    landed = lax.all_to_all(
        outgoing, ("half", "row"), split_axis=0, concat_axis=0, tiled=True
    ).reshape(2, slab_rows, n_col * cap_cols)
    row_dest = row_table.reshape(2, slab_rows)
    extra = jnp.zeros_like(parent_front)
    for child in range(2):
        spread = (
            jnp.zeros((slab_rows, col_loc), jnp.float32)
            .at[:, col_table[child]]
            .add(landed[child], mode="drop")
        )
        extra = extra.at[row_dest[child]].add(spread, mode="drop")
    assembled = parent_front + extra
    width = inverse_blocks.shape[1]
    count = inverse_blocks.shape[0]
    span = n_col // groups
    root = my_col // span
    start = my_col % span * col_loc
    factors = []
    tops = []
    for block in range(count):
        current = assembled[:, block * width : (block + 1) * width]
        if block > 0:
            earlier = jnp.concatenate(factors, axis=1)
            above = jnp.concatenate(
                [
                    tops[prior][(block - prior - 1) * width : (block - prior) * width]
                    for prior in range(block)
                ],
                axis=1,
            )
            current = current - highest_outer(earlier, above)
        result = highest_outer(current, jnp.tril(inverse_blocks[block]))
        factors.append(result)
        if block + 1 < count:
            tops.append(from_root(result[(block + 1) * width : count * width], ("half", "row"), 0))
    local_factor = jnp.concatenate(factors, axis=1)
    factor_rows = from_root(local_factor, "col", 0)
    piece = lax.dynamic_slice_in_dim(factor_rows, start, col_loc, 0)
    factor_cols = from_root(piece, ("half", "row"), root)
    updated_front = assembled - highest_outer(factor_rows, factor_cols)
    return (updated_front, factor_rows.astype(jnp.bfloat16))


def local(parent_front, child_blocks, row_maps, inverse_blocks):
    col_loc = parent_front.shape[1]
    n_col = lax.axis_size("col")
    n_row = lax.axis_size("row")
    groups = lax.axis_size("half") * n_row
    share = child_blocks.shape[2] // n_col
    panel = inverse_blocks.shape[0] * inverse_blocks.shape[1]
    args = (parent_front, child_blocks, row_maps, inverse_blocks)
    if share % LANES or groups & (groups - 1) or panel > min(parent_front.shape):
        return general(*args)
    plan = column_plan(row_maps, col_loc, n_col, share, panel)
    return lax.cond(plan[-1] <= share, lambda *given: even(*given, plan), general, *args)


def solution(mesh):
    in_specs = (P(("half", "row"), "col"), P("half", "row", "col"), P(), P())
    out_specs = (P(("half", "row"), "col"), P(("half", "row"), None))
    return jax.shard_map(local, mesh=mesh, in_specs=in_specs, out_specs=out_specs, check_vma=False)
```
